512 devices in a mesh: dp: 64 (over y, z), mp: 8 (over x, core).
Axes of the slice: x: 4, y: 8, z: 8, core: 2. Of those that a mesh axis runs over, the one named last changes fastest.
Arguments:
- hidden: bfloat16 [32768, 8192], P('dp', 'mp'), may hold values from -6 to 6
- queries: bfloat16 [32768, 4096], P('dp', 'mp'), may hold values from -6 to 6
- keys: bfloat16 [32768, 512], P('dp'), may hold values from -6 to 6
- upstream: bfloat16 [32768, 4096], P('dp', 'mp'), may hold values from -6 to 6
- value_matrix: bfloat16 [8192, 512], P(('mp', 'dp')), may hold values from -0.0625 to 0.0625
- lengths: int32 [64, 64], replicated, may hold values from 1 to 8, 256 in all within a row
- plan: int32 [64, 64], replicated, may hold values from 0 to 63, each once within a row
- correct: int32 [64, 64], P('dp'), may hold values 0 or 1
- problem: int32 [64, 64], P('dp'), may hold values from 0 to 63, as said below
Outputs:
- context: bfloat16 [16384, 4096], P('dp', 'mp')
- grad_weight: float32 [8192, 512], P(('mp', 'dp'))
The draws below stay inside these ranges and needn't reach their ends.
Inputs may be any that keep to these rules, and one draw needn't show every extreme that they name: `lengths`: each row b sums to 256; some entry equals 8. `plan`: each row is a permutation: every slot of a rollout device goes to exactly one bin. Every problem id occurs exactly 64 times.
All inputs are finite; a program needn't handle non-finite values. No bound on the sum of `correct` on one device may be relied on, other than what follows from the above.
Results may differ from the reference program's by a relative error of at most 0.02.
Values may be sent and summed in bfloat16 or wider, within the bound.
No kernel may reach another device: no remote copies, remote signals or barrier semaphores. Data moves between devices by JAX's collectives and lax.ppermute only.
A program may use at most 64 MiB of HBM per device.

```python
import math
import jax
import jax.numpy as jnp
import numpy as np
from jax import lax

MODEL_WIDTH = 8192
LOCAL_QUERY_HEADS = 32
LOCAL_KEY_HEADS = 4
HEAD_WIDTH = 128
LMAX = 8
GROUP = 64
KPASS = 8
SAMP_DEV = 64
PACKED_TOKENS = 256
ROLLOUT_TOTAL = 32768
TOKENS = 16384
NPROB = 64
N_DP = 64


def draw_keys(key, part):
    key = jax.random.fold_in(key, 1)
    return jnp.clip(jax.random.normal(key, (ROLLOUT_TOTAL, LOCAL_KEY_HEADS * HEAD_WIDTH), jnp.float32), -6.0, 6.0).astype(jnp.bfloat16)


def draw_queries(key, part):
    key = jax.random.fold_in(key, 2)
    return jnp.clip(jax.random.normal(key, (ROLLOUT_TOTAL, LOCAL_QUERY_HEADS * HEAD_WIDTH), jnp.float32), -6.0, 6.0).astype(jnp.bfloat16)


def draw_problem(key, part):
    key = jax.random.fold_in(key, 3)
    order = jax.random.permutation(key, N_DP * SAMP_DEV)
    return (order // GROUP).reshape(N_DP, SAMP_DEV).astype(jnp.int32)


def with_ends(values, stream_key, low, top_value):
    dims = values.shape
    spot = [jax.random.randint(jax.random.fold_in(stream_key, axis), (), 0, dims[axis]) for axis in range(len(dims))]
    values = values.at[tuple(spot)].set(low)
    longest = dims.index(max(dims))
    spot[longest] = (spot[longest] + 1) % dims[longest]
    return values.at[tuple(spot)].set(top_value)


def shard_levels(stream_key, shape, shards, least, largest):
    def one(dim, parts):
        heights = jax.random.uniform(jax.random.fold_in(jax.random.fold_in(stream_key, 6), dim), (parts,), jnp.float32, least / len(shards), largest / len(shards))
        return jnp.repeat(jnp.exp(heights), shape[dim] // parts).reshape((-1,) + (1,) * (len(shape) - dim - 1))

    factor_of = one(*shards[0])
    for cut in shards[1:]:
        factor_of = factor_of * one(*cut)
    return factor_of


def profile(count, total, bound, skew):
    weights = [(1 << 20) // math.isqrt(rank ** skew) + 1 for rank in range(2, count + 1)]
    spare, given = total - bound - (count - 1), [1] * (count - 1)
    while spare > 0:
        movable = [i for i in range(count - 1) if given[i] < bound]
        mass, remaining = sum([weights[i] for i in movable]), spare
        for i in movable:
            extra = min(bound - given[i], max(1, remaining * weights[i] // mass), spare)
            given[i] = given[i] + extra
            spare = spare - extra
    return np.array([bound] + given)


def ragged(own_key, number_of, total, reach, slope):
    if number_of == 2:
        one = jax.random.randint(own_key, (), max(1, total - reach), min(reach, total - 1) + 1)
        return jnp.stack([one, total - one])
    sizes = jnp.asarray(profile(number_of, total, reach, slope), jnp.int32)
    couples = (number_of - 1) // 2
    giver, sink = sizes[1:1 + 2 * couples:2], sizes[2:2 + 2 * couples:2]
    room = jnp.minimum(giver - 1, reach - sink)
    shifted = jax.random.randint(jax.random.fold_in(own_key, 1), (couples,), 0, 1 << 20) % (room + 1)
    sizes = sizes.at[1:1 + 2 * couples:2].set(giver - shifted).at[2:2 + 2 * couples:2].set(sink + shifted)
    return sizes[jax.random.permutation(jax.random.fold_in(own_key, 2), number_of)]


def gaussian(key, dims, deviation, limit, cuts=(), kind=jnp.bfloat16):
    result = jax.random.normal(key, dims, jnp.float32) * deviation
    if len(cuts) > 0:
        result = shard_levels(key, dims, cuts, -0.22, 0.18) * result
    return jnp.clip(result, min=-limit, max=limit).astype(kind)


def setup_inputs(seed: int = 0) -> dict:
    seeds = jax.random.split(jax.random.key(seed), 10)
    hidden = gaussian(seeds[0], (ROLLOUT_TOTAL, MODEL_WIDTH), 1.0, 6.0, ((0, 64), (1, 8)))
    queries = draw_queries(jax.random.fold_in(seeds[9], 71), 0)
    keys = draw_keys(jax.random.fold_in(seeds[9], 71), 0)
    upstream = gaussian(seeds[3], (ROLLOUT_TOTAL, LOCAL_QUERY_HEADS * HEAD_WIDTH), 1.0, 6.0, ((0, 64), (1, 8)))
    value_matrix = gaussian(seeds[4], (MODEL_WIDTH, LOCAL_KEY_HEADS * HEAD_WIDTH), MODEL_WIDTH ** -0.5, 0.0625, ((0, 512),))
    lengths = jax.vmap(lambda own: ragged(own, SAMP_DEV, PACKED_TOKENS, LMAX, 2))(jax.random.split(seeds[5], N_DP)).reshape((N_DP, SAMP_DEV)).astype(jnp.int32)
    plan = jax.vmap(lambda own: jax.random.permutation(own, SAMP_DEV))(jax.random.split(seeds[6], N_DP)).reshape((N_DP, SAMP_DEV)).astype(jnp.int32)
    correct = with_ends((jax.random.randint(seeds[7], (N_DP, SAMP_DEV), 0, 8) < 1).astype(jnp.int32), jax.random.fold_in(seeds[7], 1), 0, 1)
    problem = draw_problem(jax.random.fold_in(seeds[9], 71), 0)
    return dict(hidden=hidden, queries=queries, keys=keys, upstream=upstream, value_matrix=value_matrix, lengths=lengths, plan=plan, correct=correct, problem=problem)


def pass_rate(total, hits):
    missed = jnp.ones_like(hits)
    for step in range(KPASS):
        missed = missed * jnp.maximum(total - hits - step, 0.0) / (total - step)
    return 1.0 - missed

def advantage_table(correct, problem):
    flat_ok = correct.reshape(-1).astype(jnp.float32)
    flat_id = problem.reshape(-1).astype(jnp.int32)
    counts = jax.ops.segment_sum(flat_ok, flat_id, num_segments=NPROB)
    own = counts[flat_id]
    return pass_rate(float(GROUP), own) - pass_rate(float(GROUP - 1), own - flat_ok)

def layout(lengths, plan):
    ends = jnp.cumsum(lengths, axis=1).astype(jnp.int32)
    starts = (ends - lengths).astype(jnp.int32)
    token_rows = jnp.arange(PACKED_TOKENS, dtype=jnp.int32)
    slot = lax.optimization_barrier(jnp.sum((token_rows[None, :, None] >= ends[:, None, :]).astype(jnp.int32), axis=2)).astype(jnp.int32)
    place = (token_rows[None, :] - jnp.take_along_axis(starts, slot, axis=1)).astype(jnp.int32)
    local = jnp.take_along_axis(plan.T.astype(jnp.int32), slot, axis=1).astype(jnp.int32)
    return (slot, place, local)

def reference(hidden, queries, keys, upstream, value_matrix, lengths, plan, correct, problem):
    slot, place, local = layout(lengths, plan)
    sample = (slot * SAMP_DEV + local).astype(jnp.int32)
    source_row = (sample * LMAX + place).astype(jnp.int32)
    gain = advantage_table(correct, problem)
    row_gain = gain[sample]
    head_groups = LOCAL_QUERY_HEADS // LOCAL_KEY_HEADS
    factor = 1.0 / math.sqrt(HEAD_WIDTH)

    def one_bin(total, inputs):
        token_rows, segment, position, weight = inputs
        x_rows = hidden[token_rows]
        value_tensor = jnp.dot(x_rows, value_matrix, preferred_element_type=jnp.float32).astype(jnp.bfloat16)
        query = queries[token_rows].reshape(PACKED_TOKENS, LOCAL_QUERY_HEADS, HEAD_WIDTH).astype(jnp.float32)
        key_slice = jnp.repeat(keys[token_rows].reshape(PACKED_TOKENS, LOCAL_KEY_HEADS, HEAD_WIDTH), head_groups, axis=1).astype(jnp.float32)
        value_slice = jnp.repeat(value_tensor.reshape(PACKED_TOKENS, LOCAL_KEY_HEADS, HEAD_WIDTH), head_groups, axis=1).astype(jnp.float32)
        scores = jnp.einsum('qhd,khd->hqk', query, key_slice) * factor
        allowed = (segment[:, None] == segment[None, :]) & (position[None, :] <= position[:, None])
        scores = jnp.where(allowed[None], scores, -jnp.inf)
        top = lax.optimization_barrier(jnp.max(scores, axis=2, keepdims=True))
        expo = jnp.exp(scores - top)
        probs = (expo / lax.optimization_barrier(jnp.sum(expo, axis=2, keepdims=True))).astype(jnp.bfloat16)
        context = jnp.einsum('hqk,khd->qhd', probs.astype(jnp.float32), value_slice).astype(jnp.bfloat16)
        grad_ctx = (weight[:, None] * upstream[token_rows].astype(jnp.float32)).astype(jnp.bfloat16)
        grad_ctx = grad_ctx.reshape(PACKED_TOKENS, LOCAL_QUERY_HEADS, HEAD_WIDTH).astype(jnp.float32)
        head_gradient = jnp.einsum('hqk,qhd->khd', probs.astype(jnp.float32), grad_ctx)
        value_gradient = head_gradient.reshape(PACKED_TOKENS, LOCAL_KEY_HEADS, head_groups, HEAD_WIDTH).sum(axis=2).reshape(PACKED_TOKENS, LOCAL_KEY_HEADS * HEAD_WIDTH).astype(jnp.bfloat16)
        total = total + lax.dot_general(x_rows, value_gradient, (((0,), (0,)), ((), ())), preferred_element_type=jnp.float32)
        return (total, context.reshape(PACKED_TOKENS, LOCAL_QUERY_HEADS * HEAD_WIDTH))
    start_offset = jnp.zeros((MODEL_WIDTH, LOCAL_KEY_HEADS * HEAD_WIDTH), jnp.float32)
    grad_weight, context = lax.scan(one_bin, start_offset, (source_row, slot, place, row_gain))
    return (context.reshape(TOKENS, LOCAL_QUERY_HEADS * HEAD_WIDTH), grad_weight)
```

```python
import math

import jax
import jax.numpy as jnp
from jax import lax
from jax.experimental import pallas as pl
from jax.experimental.pallas import tpu as pltpu
from jax.sharding import PartitionSpec as P

KEY_HEADS = 4
HEAD = 128
HEADS_DEV = 4
LMAX = 8
GROUP = 64
KPASS = 8
BINS = 64
ROWS = 512
PACKED = 256
FEATS = 1024
WROWS = 16
BLOCK = KEY_HEADS * WROWS
EXTRA = 8
TILE = 128

f32 = jnp.float32
bf16 = jnp.bfloat16
VM = pl.BlockSpec(memory_space=pltpu.VMEM)
SM = pl.BlockSpec(memory_space=pltpu.SMEM)
PARAMS = pltpu.CompilerParams(vmem_limit_bytes=40 * 1024 * 1024)


def iota(shape, dim):
    return lax.broadcasted_iota(jnp.int32, shape, dim)


def dot(a, b, dims=((1,), (0,))):
    return lax.dot_general(a, b, (dims, ((), ())), preferred_element_type=f32)


def call(body, out_shape, args, specs, flops=0, moved=0):
    return pl.pallas_call(
        body,
        out_shape=out_shape,
        in_specs=specs,
        out_specs=jax.tree.map(lambda _: VM, out_shape),
        compiler_params=PARAMS,
        cost_estimate=pl.CostEstimate(flops=flops, bytes_accessed=moved, transcendentals=0),
    )(*args)


def weight_block(wm_ref, ok_ref, id_ref, out_ref):
    member = (id_ref[...] == iota((128, BINS), 0) % BINS).astype(f32).astype(bf16)
    ok = jnp.broadcast_to(ok_ref[...], (EXTRA, BINS)).astype(f32).astype(bf16)
    hits = dot(ok, member, ((1,), (1,))).astype(bf16)
    for m in range(KEY_HEADS):
        out_ref[:, m * WROWS : (m + 1) * WROWS, :] = jnp.broadcast_to(
            wm_ref[:, m * HEAD : (m + 1) * HEAD][None], (BINS, WROWS, HEAD)
        )
    out_ref[:, BLOCK:, :] = jnp.broadcast_to(hits[None], (BINS, EXTRA, HEAD))


def attend(
    where_ref, x_ref, q_ref, k_ref, g_ref, len_ref, plan_ref, ok_ref, id_ref,
    xb_ref, xt_ref, dv_ref, pr_ref, pick_ref,
):
    me, xpos = where_ref[0], where_ref[1]
    sample = (iota((ROWS, BINS), 0) // LMAX == iota((ROWS, BINS), 1)).astype(f32).astype(bf16)
    mine = iota((ROWS, BINS), 1) == me
    lens = dot(sample, len_ref[...].astype(f32).astype(bf16))
    lens = jnp.sum(jnp.where(mine, lens, 0.0), axis=1, keepdims=True)
    slot = dot(sample, plan_ref[...].astype(f32).astype(bf16), ((1,), (1,)))
    slot = jnp.sum(jnp.where(mine, slot, 0.0), axis=1, keepdims=True)
    slot = slot.astype(jnp.int32)
    source = slot == iota((ROWS, BINS), 1)
    prob_id = jnp.sum(jnp.where(source, id_ref[...], 0).astype(f32), axis=1, keepdims=True)
    good = jnp.sum(jnp.where(source, ok_ref[...], 0).astype(f32), axis=1, keepdims=True)
    lane = (prob_id + BINS * good).astype(jnp.int32)
    pick_ref[...] = (lane == iota((ROWS, 128), 1)).astype(f32)
    row_source = slot * LMAX + iota((ROWS, 1), 0) % LMAX
    order = (row_source == iota((ROWS, ROWS), 1)).astype(f32).astype(bf16)
    valid = (iota((ROWS, 1), 0) % LMAX).astype(f32) < lens
    queries = dot(order, q_ref[...]).astype(bf16)
    cotangents = dot(order, g_ref[...]).astype(bf16)
    keys = dot(order, k_ref[:, pl.ds(pl.multiple_of(xpos * HEAD, HEAD), HEAD)]).astype(bf16)
    r, c = iota((TILE, TILE), 0), iota((TILE, TILE), 1)
    allowed = (r // LMAX == c // LMAX) & (c <= r)
    allowed = jnp.concatenate([allowed] * HEADS_DEV, axis=0)
    for tile in range(ROWS // TILE):
        rows = slice(tile * TILE, (tile + 1) * TILE)
        stack = lambda a: jnp.concatenate(
            [a[rows, h * HEAD : (h + 1) * HEAD] for h in range(HEADS_DEV)], axis=0
        )
        scores = dot(stack(queries), keys[rows], ((1,), (1,))) * (1.0 / math.sqrt(HEAD))
        scores = jnp.where(allowed, scores, -jnp.inf)
        expo = jnp.exp(scores - jnp.max(scores, axis=1, keepdims=True))
        probs = expo / jnp.sum(expo, axis=1, keepdims=True)
        alive = jnp.concatenate([valid[rows]] * HEADS_DEV, axis=0)
        probs = jnp.where(alive, probs, 0.0).astype(bf16)
        dv_ref[rows, :] = dot(probs, stack(cotangents), ((0,), (0,))).astype(bf16)
        short = jnp.zeros((TILE, HEAD), f32)
        for h in range(HEADS_DEV):
            to = (c == h * LMAX + r % LMAX).astype(f32).astype(bf16)
            short += dot(probs[h * TILE : (h + 1) * TILE], to)
        pr_ref[rows, :] = short.astype(bf16)
    x_bins = dot(order, x_ref[...]).astype(bf16)
    xb_ref[...] = x_bins
    xt_ref[...] = x_bins.T


def pass_rate(total, hits):
    missed = jnp.ones_like(hits)
    for step in range(KPASS):
        missed = missed * jnp.maximum(total - hits - step, 0.0) / (total - step)
    return 1.0 - missed


def weight_gradient(where_ref, w_ref, xt_ref, d0_ref, d1_ref, d2_ref, d3_ref, pick_ref, pr_ref, out_ref):
    xpos = where_ref[1]
    hits = jnp.sum(w_ref[:, BLOCK:, :].astype(f32), axis=0)[:1]
    good = (iota((1, 128), 1) // BINS).astype(f32)
    table = pass_rate(float(GROUP), hits) - pass_rate(float(GROUP - 1), hits - good)
    gain = jnp.sum(pick_ref[...] * table, axis=1, keepdims=True)
    dv = jnp.concatenate(
        [(gain * d[...].astype(f32)).astype(bf16) for d in (d0_ref, d1_ref, d2_ref, d3_ref)], axis=1
    )
    grad = dot(xt_ref[...], dv).astype(bf16)
    for i in range(KEY_HEADS):
        m = lax.rem(xpos + KEY_HEADS - i, KEY_HEADS)
        out_ref[:, pl.ds(pl.multiple_of(m * WROWS, WROWS), WROWS), :] = grad[
            :, i * HEAD : (i + 1) * HEAD
        ].reshape(BINS, WROWS, HEAD)
    out_ref[:, BLOCK:, :] = pr_ref[...].reshape(BINS, LMAX, HEAD)


def project(where_ref, w_ref, xb_ref, out_ref):
    xpos = where_ref[1]
    for i in range(KEY_HEADS):
        m = lax.rem(xpos + i, KEY_HEADS)
        w = w_ref[:, pl.ds(pl.multiple_of(m * WROWS, WROWS), WROWS), :].reshape(FEATS, HEAD)
        out_ref[i] = dot(xb_ref[...], w).astype(bf16)


def collect(where_ref, got_ref, len_ref, grad_ref, mix_ref):
    me = where_ref[0]
    total = jnp.sum(got_ref[:, :BLOCK, :].astype(f32), axis=0)
    for m in range(KEY_HEADS):
        grad_ref[:, m * HEAD : (m + 1) * HEAD] = total[m * WROWS : (m + 1) * WROWS]
    probs = got_ref[:, BLOCK:, :].reshape(ROWS, HEAD)
    own = jnp.where(iota((BINS, BINS), 0) == me, len_ref[...], 0).astype(f32)
    own = jnp.broadcast_to(jnp.sum(own, axis=0, keepdims=True), (8, BINS)).astype(bf16)
    s, lane = iota((BINS, ROWS), 0), iota((BINS, ROWS), 1)
    start = dot(own, (s < lane // LMAX).astype(f32).astype(bf16))[:1].astype(jnp.int32)
    size = dot(own, (s == lane // LMAX).astype(f32).astype(bf16))[:1].astype(jnp.int32)
    i, lane = iota((PACKED, ROWS), 0), iota((PACKED, ROWS), 1)
    same = (i >= start) & (i < start + size)
    take = same & (i == start + lane % LMAX)
    packed = dot(take.astype(f32).astype(bf16), probs).astype(bf16)
    a, b = iota((HEAD, ROWS), 0), iota((HEAD, ROWS), 1)
    for h in range(HEADS_DEV):
        spread = dot(packed, (a == h * LMAX + b % LMAX).astype(f32).astype(bf16))
        mix_ref[h * PACKED : (h + 1) * PACKED, :] = jnp.where(same, spread, 0.0).astype(bf16)


def mix(mix_ref, v_ref, out_ref):
    context = dot(mix_ref[...], v_ref[...]).astype(bf16)
    for h in range(HEADS_DEV):
        out_ref[:, h * HEAD : (h + 1) * HEAD] = context[h * PACKED : (h + 1) * PACKED]


def swap_cores(a):
    return lax.ppermute(a, "mp", [(p, p ^ 1) for p in range(8)])


def shift_x(a, step):
    return lax.ppermute(a, "mp", [(p, (p + 2 * step) % 8) for p in range(8)])


def all_to_all(a):
    return lax.all_to_all(a, "dp", split_axis=0, concat_axis=0, tiled=True)


def per_device(hidden, queries, keys, upstream, value_matrix, lengths, plan, correct, problem):
    where = jnp.stack([lax.axis_index("dp"), lax.axis_index("mp") // 2]).astype(jnp.int32)
    struct = jax.ShapeDtypeStruct
    block = struct((BINS, BLOCK + EXTRA, HEAD), bf16)
    sent = call(weight_block, block, (value_matrix, correct, problem), [VM] * 3, 10**6, 10**6)
    weights = all_to_all(sent)
    x_bins, x_turned, dv, probs, pick = call(
        attend,
        (
            struct((ROWS, FEATS), bf16),
            struct((FEATS, ROWS), bf16),
            struct((ROWS, HEAD), bf16),
            struct((ROWS, HEAD), bf16),
            struct((ROWS, 128), f32),
        ),
        (where, hidden, queries, keys, upstream, lengths, plan, correct, problem),
        [SM] + [VM] * 8,
        2 * 10**9,
        5 * 10**6,
    )
    dv = (dv.astype(f32) + swap_cores(dv).astype(f32)).astype(bf16)
    others = [shift_x(dv, step) for step in (1, 2, 3)]
    grads = call(
        weight_gradient,
        block,
        (where, weights, x_turned, dv, *others, pick, probs),
        [SM] + [VM] * 8,
        6 * 10**8,
        4 * 10**6,
    )
    got = all_to_all(grads)
    part = call(
        project,
        struct((KEY_HEADS, ROWS, HEAD), bf16),
        (where, weights, x_bins),
        [SM] + [VM] * 2,
        6 * 10**8,
        3 * 10**6,
    )
    both = part.astype(f32) + swap_cores(part).astype(f32)
    value = both[0]
    for step in (1, 2, 3):
        value = value + shift_x(both[step].astype(bf16), step).astype(f32)
    arrived = all_to_all(value.astype(bf16).reshape(BINS, LMAX, HEAD))
    grad_weight, matrix = call(
        collect,
        (struct((WROWS, KEY_HEADS * HEAD), f32), struct((HEADS_DEV * PACKED, ROWS), bf16)),
        (where, got, lengths),
        [SM] + [VM] * 2,
        6 * 10**8,
        3 * 10**6,
    )
    context = call(
        mix,
        struct((PACKED, HEADS_DEV * HEAD), bf16),
        (matrix, arrived.reshape(ROWS, HEAD)),
        [VM] * 2,
        3 * 10**8,
        2 * 10**6,
    )
    return context, grad_weight


def solution(mesh):
    in_specs = (
        P("dp", "mp"),
        P("dp", "mp"),
        P("dp", None),
        P("dp", "mp"),
        P(("mp", "dp"), None),
        P(),
        P(),
        P("dp", None),
        P("dp", None),
    )
    out_specs = (P("dp", "mp"), P(("mp", "dp"), None))
    return jax.shard_map(
        per_device, mesh=mesh, in_specs=in_specs, out_specs=out_specs, check_vma=False
    )
```

```python
import math

import jax
import jax.numpy as jnp
from jax import lax
from jax.experimental import pallas as pl
from jax.experimental.pallas import tpu as pltpu
from jax.sharding import PartitionSpec as P

KEY_HEADS = 4
HEAD = 128
HEADS_DEV = 4
LMAX = 8
GROUP = 64
KPASS = 8
BINS = 64
ROWS = 512
PACKED = 256
FEATS = 1024
WROWS = 16
BLOCK = KEY_HEADS * WROWS
EXTRA = 8
TILE = 128

f32 = jnp.float32
bf16 = jnp.bfloat16
VM = pl.BlockSpec(memory_space=pltpu.VMEM)
SM = pl.BlockSpec(memory_space=pltpu.SMEM)
HB = pl.BlockSpec(memory_space=pltpu.HBM)
MIB = 1024 * 1024
ATTEND_MIB = 60


def iota(shape, dim):
    return lax.broadcasted_iota(jnp.int32, shape, dim)


def dot(a, b, dims=((1,), (0,))):
    return lax.dot_general(a, b, (dims, ((), ())), preferred_element_type=f32)


def call(body, out_shape, args, specs, flops=0, moved=0, vmem=16, scratch=()):
    return pl.pallas_call(
        body,
        out_shape=out_shape,
        in_specs=specs,
        out_specs=jax.tree.map(lambda _: VM, out_shape),
        scratch_shapes=scratch,
        compiler_params=pltpu.CompilerParams(vmem_limit_bytes=vmem * MIB),
        cost_estimate=pl.CostEstimate(flops=flops, bytes_accessed=moved, transcendentals=0),
    )(*args)


def fetch(sources, targets, sems):
    copies = [pltpu.make_async_copy(s, t, sems.at[i]) for i, (s, t) in enumerate(zip(sources, targets))]
    for copy in copies:
        copy.start()
    return copies


def weight_block(wm_hbm, ok_hbm, id_hbm, out_ref, wm_ref, ok_ref, id_ref, sems):
    for copy in fetch((wm_hbm, ok_hbm, id_hbm), (wm_ref, ok_ref, id_ref), sems):
        copy.wait()
    member = (id_ref[...] == iota((128, BINS), 0) % BINS).astype(f32).astype(bf16)
    ok = jnp.broadcast_to(ok_ref[...], (EXTRA, BINS)).astype(f32).astype(bf16)
    hits = dot(ok, member, ((1,), (1,))).astype(bf16)
    for m in range(KEY_HEADS):
        out_ref[:, m * WROWS : (m + 1) * WROWS, :] = jnp.broadcast_to(
            wm_ref[:, m * HEAD : (m + 1) * HEAD][None], (BINS, WROWS, HEAD)
        )
    out_ref[:, BLOCK:, :] = jnp.broadcast_to(hits[None], (BINS, EXTRA, HEAD))


def slots(me, plan_ref):
    sample = (iota((ROWS, BINS), 0) // LMAX == iota((ROWS, BINS), 1)).astype(f32).astype(bf16)
    slot = dot(sample, plan_ref[...].astype(f32).astype(bf16), ((1,), (1,)))
    slot = jnp.sum(jnp.where(iota((ROWS, BINS), 1) == me, slot, 0.0), axis=1, keepdims=True)
    return sample, slot.astype(jnp.int32)


def reorder(slot):
    source = slot * LMAX + iota((ROWS, 1), 0) % LMAX
    return (source == iota((ROWS, ROWS), 1)).astype(f32).astype(bf16)


def attend(where_ref, q_hbm, k_hbm, g_hbm, len_ref, plan_ref, dv_ref, pr_ref, q_ref, k_ref, g_ref, sems):
    me, xpos = where_ref[0], where_ref[1]
    key_columns = k_hbm.at[:, pl.ds(pl.multiple_of(xpos * HEAD, HEAD), HEAD)]
    got_q, got_k, got_g = fetch((q_hbm, key_columns, g_hbm), (q_ref, k_ref, g_ref), sems)
    sample, slot = slots(me, plan_ref)
    lens = dot(sample, len_ref[...].astype(f32).astype(bf16))
    lens = jnp.sum(jnp.where(iota((ROWS, BINS), 1) == me, lens, 0.0), axis=1, keepdims=True)
    valid = (iota((ROWS, 1), 0) % LMAX).astype(f32) < lens
    order = reorder(slot)
    got_q.wait()
    queries = dot(order, q_ref[...]).astype(bf16)
    got_k.wait()
    keys = dot(order, k_ref[...]).astype(bf16)
    got_g.wait()
    cotangents = dot(order, g_ref[...]).astype(bf16)
    r, c = iota((TILE, TILE), 0), iota((TILE, TILE), 1)
    allowed = (r // LMAX == c // LMAX) & (c <= r)
    allowed = jnp.concatenate([allowed] * HEADS_DEV, axis=0)
    for tile in range(ROWS // TILE):
        rows = slice(tile * TILE, (tile + 1) * TILE)
        stack = lambda a: jnp.concatenate(
            [a[rows, h * HEAD : (h + 1) * HEAD] for h in range(HEADS_DEV)], axis=0
        )
        scores = dot(stack(queries), keys[rows], ((1,), (1,))) * (1.0 / math.sqrt(HEAD))
        scores = jnp.where(allowed, scores, -jnp.inf)
        expo = jnp.exp(scores - jnp.max(scores, axis=1, keepdims=True))
        probs = expo / jnp.sum(expo, axis=1, keepdims=True)
        alive = jnp.concatenate([valid[rows]] * HEADS_DEV, axis=0)
        probs = jnp.where(alive, probs, 0.0).astype(bf16)
        dv_ref[rows, :] = dot(probs, stack(cotangents), ((0,), (0,))).astype(bf16)
        short = jnp.zeros((TILE, HEAD), f32)
        for h in range(HEADS_DEV):
            to = (c == h * LMAX + r % LMAX).astype(f32).astype(bf16)
            short += dot(probs[h * TILE : (h + 1) * TILE], to)
        pr_ref[rows, :] = short.astype(bf16)


def put_in_order(where_ref, x_ref, plan_ref, ok_ref, id_ref, dv_ref, xb_ref, out_ref):
    _, slot = slots(where_ref[0], plan_ref)
    xb_ref[...] = dot(reorder(slot), x_ref[...]).astype(bf16)
    source = slot == iota((ROWS, BINS), 1)
    lane = jnp.where(source, id_ref[...] + BINS * ok_ref[...], 0).astype(f32)
    lane = jnp.sum(lane, axis=1, keepdims=True).astype(jnp.int32)
    for m in range(KEY_HEADS):
        out_ref[:, m * HEAD : (m + 1) * HEAD] = dv_ref[m]
    out_ref[:, KEY_HEADS * HEAD :] = (lane == iota((ROWS, HEAD), 1)).astype(f32).astype(bf16)


def pass_rate(total, hits):
    missed = jnp.ones_like(hits)
    for step in range(KPASS):
        missed = missed * jnp.maximum(total - hits - step, 0.0) / (total - step)
    return 1.0 - missed


def multiply(where_ref, w_ref, xb_ref, dv_ref, part_ref, grad_ref):
    xpos = where_ref[1]
    for i in range(KEY_HEADS):
        m = lax.rem(xpos + i, KEY_HEADS)
        w = w_ref[:, pl.ds(pl.multiple_of(m * WROWS, WROWS), WROWS), :].reshape(FEATS, HEAD)
        part_ref[i] = dot(xb_ref[...], w).astype(bf16)
    hits = jnp.sum(w_ref[:, BLOCK:, :].astype(f32), axis=0)[:1]
    good = (iota((1, 128), 1) // BINS).astype(f32)
    table = pass_rate(float(GROUP), hits) - pass_rate(float(GROUP - 1), hits - good)
    pick = dv_ref[:, KEY_HEADS * HEAD :].astype(f32)
    gain = jnp.sum(pick * table, axis=1, keepdims=True)
    dv = (gain * dv_ref[:, : KEY_HEADS * HEAD].astype(f32)).astype(bf16)
    grad = dot(xb_ref[...].T, dv).astype(bf16)
    for m in range(KEY_HEADS):
        grad_ref[m] = grad[:, m * HEAD : (m + 1) * HEAD]


def add_cores(where_ref, mine_ref, other_ref, own_ref, next_ref, far_ref):
    core = where_ref[2]
    half = pl.ds(pl.multiple_of(core * (ROWS // 2), ROWS // 2), ROWS // 2)
    own_ref[...] = mine_ref[0].astype(f32) + other_ref[0].astype(f32)
    to = 1 + 2 * core
    next_ref[...] = (mine_ref[to].astype(f32) + other_ref[to].astype(f32)).astype(bf16)
    far_ref[...] = (mine_ref[2, half].astype(f32) + other_ref[2, half].astype(f32)).astype(bf16)


def add_arrived(where_ref, next_ref, far_ref, out_ref):
    half = pl.ds(pl.multiple_of(where_ref[2] * (ROWS // 2), ROWS // 2), ROWS // 2)
    out_ref[...] = next_ref[...]
    out_ref[half] = (next_ref[half].astype(f32) + far_ref[...].astype(f32)).astype(bf16)


def assemble(own_ref, r1_ref, r2_ref, near_ref, pr_ref, out_ref):
    grad = jnp.sum(near_ref[...].astype(f32), axis=0).astype(bf16)
    out_ref[:, :WROWS, :] = grad.reshape(BINS, WROWS, HEAD)
    value = own_ref[...] + r1_ref[...].astype(f32) + r2_ref[...].astype(f32)
    out_ref[:, WROWS : WROWS + LMAX, :] = value.astype(bf16).reshape(BINS, LMAX, HEAD)
    out_ref[:, WROWS + LMAX :, :] = pr_ref[...].reshape(BINS, LMAX, HEAD)


def finish(where_ref, got_ref, len_ref, grad_ref, out_ref):
    me = where_ref[0]
    probs = got_ref[:, WROWS + LMAX :, :].reshape(ROWS, HEAD)
    values = got_ref[:, WROWS : WROWS + LMAX, :].reshape(ROWS, HEAD)
    own = jnp.where(iota((BINS, BINS), 0) == me, len_ref[...], 0).astype(f32)
    own = jnp.broadcast_to(jnp.sum(own, axis=0, keepdims=True), (8, BINS)).astype(bf16)
    s, lane = iota((BINS, ROWS), 0), iota((BINS, ROWS), 1)
    start = dot(own, (s < lane // LMAX).astype(f32).astype(bf16))[:1].astype(jnp.int32)
    size = dot(own, (s == lane // LMAX).astype(f32).astype(bf16))[:1].astype(jnp.int32)
    i, lane = iota((PACKED, ROWS), 0), iota((PACKED, ROWS), 1)
    same = (i >= start) & (i < start + size)
    take = same & (i == start + lane % LMAX)
    packed = dot(take.astype(f32).astype(bf16), probs).astype(bf16)
    a, b = iota((HEAD, ROWS), 0), iota((HEAD, ROWS), 1)
    for h in range(HEADS_DEV):
        spread = dot(packed, (a == h * LMAX + b % LMAX).astype(f32).astype(bf16))
        spread = jnp.where(same, spread, 0.0).astype(bf16)
        out_ref[:, h * HEAD : (h + 1) * HEAD] = dot(spread, values).astype(bf16)
    for m in range(KEY_HEADS):
        total = jnp.zeros((WROWS, HEAD), f32)
        for source in range(BINS):
            if square_place(source) == m:
                total += got_ref[source, :WROWS, :].astype(f32)
        grad_ref[:, m * HEAD : (m + 1) * HEAD] = total


def square_place(source):
    return source // 8 % 2 * 2 + source % 2


SQUARES = [
    [(y + i) * 8 + z + j for i in range(2) for j in range(2)]
    for y in range(0, 8, 2)
    for z in range(0, 8, 2)
]


def swap_cores(a):
    return lax.ppermute(a, "mp", [(p, p ^ 1) for p in range(8)])


def to_next_chips(a):
    return lax.ppermute(a, "mp", [(p, (p + (2, -2)[p % 2]) % 8) for p in range(8)])


def to_far_chip(a):
    return lax.ppermute(a, "mp", [(p, (p + 4) % 8) for p in range(8)])


def all_to_all(a, groups=None):
    return lax.all_to_all(
        a, "dp", split_axis=0, concat_axis=0, tiled=True, axis_index_groups=groups
    )


def per_device(hidden, queries, keys, upstream, value_matrix, lengths, plan, correct, problem):
    part_of_mp = lax.axis_index("mp")
    where = jnp.stack([lax.axis_index("dp"), part_of_mp // 2, part_of_mp % 2]).astype(jnp.int32)
    struct = jax.ShapeDtypeStruct
    rows = struct((ROWS, HEAD), bf16)
    sent = call(
        weight_block,
        struct((BINS, BLOCK + EXTRA, HEAD), bf16),
        (value_matrix, correct, problem),
        [HB] * 3,
        10**6,
        10**6,
        scratch=[
            pltpu.VMEM((WROWS, KEY_HEADS * HEAD), bf16),
            pltpu.VMEM((1, BINS), jnp.int32),
            pltpu.VMEM((1, BINS), jnp.int32),
            pltpu.SemaphoreType.DMA((3,)),
        ],
        vmem=60,
    )
    weights = all_to_all(sent)
    dv, probs = call(
        attend,
        (rows, rows),
        (where, queries, keys, upstream, lengths, plan),
        [SM] + [HB] * 3 + [VM] * 2,
        2 * 10**9,
        2 * 10**6,
        scratch=[
            pltpu.VMEM((ROWS, HEADS_DEV * HEAD), bf16),
            pltpu.VMEM((ROWS, HEAD), bf16),
            pltpu.VMEM((ROWS, HEADS_DEV * HEAD), bf16),
            pltpu.SemaphoreType.DMA((3,)),
        ],
        vmem=ATTEND_MIB,
    )
    dv = (dv.astype(f32) + swap_cores(dv).astype(f32)).astype(bf16)
    dv = lax.all_gather(dv, "mp", axis_index_groups=[[0, 2, 4, 6], [1, 3, 5, 7]])
    x_bins, packed = call(
        put_in_order,
        (struct((ROWS, FEATS), bf16), struct((ROWS, (KEY_HEADS + 1) * HEAD), bf16)),
        (where, hidden, plan, correct, problem, dv),
        [SM] + [VM] * 5,
        6 * 10**8,
        4 * 10**6,
    )
    part, grads = call(
        multiply,
        (struct((KEY_HEADS, ROWS, HEAD), bf16), struct((KEY_HEADS, FEATS, HEAD), bf16)),
        (where, weights, x_bins, packed),
        [SM] + [VM] * 3,
        10**9,
        6 * 10**6,
    )
    other_part = swap_cores(part)
    near = all_to_all(grads, SQUARES)
    own, following, far = call(
        add_cores,
        (struct((ROWS, HEAD), f32), rows, struct((ROWS // 2, HEAD), bf16)),
        (where, part, other_part),
        [SM] + [VM] * 2,
        10**6,
        2 * 10**6,
    )
    arrived = call(
        add_arrived,
        rows,
        (where, to_next_chips(following), to_far_chip(far)),
        [SM] + [VM] * 2,
        10**6,
        10**6,
    )
    block = call(
        assemble,
        struct((BINS, WROWS + 2 * LMAX, HEAD), bf16),
        (own, arrived, swap_cores(arrived), near, probs),
        [VM] * 5,
        10**6,
        3 * 10**6,
    )
    grad_weight, context = call(
        finish,
        (struct((WROWS, KEY_HEADS * HEAD), f32), struct((PACKED, HEADS_DEV * HEAD), bf16)),
        (where, all_to_all(block), lengths),
        [SM] + [VM] * 2,
        6 * 10**8,
        10**6,
    )
    return context, grad_weight


def solution(mesh):
    in_specs = (
        P("dp", "mp"),
        P("dp", "mp"),
        P("dp", None),
        P("dp", "mp"),
        P(("mp", "dp"), None),
        P(),
        P(),
        P("dp", None),
        P("dp", None),
    )
    out_specs = (P("dp", "mp"), P(("mp", "dp"), None))
    return jax.shard_map(
        per_device, mesh=mesh, in_specs=in_specs, out_specs=out_specs, check_vma=False
    )
```

```python
import math

import jax
import jax.numpy as jnp
from jax import lax
from jax.experimental import pallas as pl
from jax.experimental.pallas import tpu as pltpu
from jax.sharding import PartitionSpec as P

KEY_HEADS = 4
HEAD = 128
HEADS_DEV = 4
LMAX = 8
GROUP = 64
KPASS = 8
BINS = 64
ROWS = 512
PACKED = 256
FEATS = 1024
WROWS = 16
BLOCK = KEY_HEADS * WROWS
EXTRA = 8
TILE = 128

f32 = jnp.float32
bf16 = jnp.bfloat16
VM = pl.BlockSpec(memory_space=pltpu.VMEM)
SM = pl.BlockSpec(memory_space=pltpu.SMEM)
HB = pl.BlockSpec(memory_space=pltpu.HBM)
MIB = 1024 * 1024
ATTEND_MIB = 60


def iota(shape, dim):
    return lax.broadcasted_iota(jnp.int32, shape, dim)


def dot(a, b, dims=((1,), (0,))):
    return lax.dot_general(a, b, (dims, ((), ())), preferred_element_type=f32)


def call(body, out_shape, args, specs, flops=0, moved=0, vmem=16, scratch=()):
    return pl.pallas_call(
        body,
        out_shape=out_shape,
        in_specs=specs,
        out_specs=jax.tree.map(lambda _: VM, out_shape),
        scratch_shapes=scratch,
        compiler_params=pltpu.CompilerParams(vmem_limit_bytes=vmem * MIB),
        cost_estimate=pl.CostEstimate(flops=flops, bytes_accessed=moved, transcendentals=0),
    )(*args)


def fetch(sources, targets, sems):
    copies = [pltpu.make_async_copy(s, t, sems.at[i]) for i, (s, t) in enumerate(zip(sources, targets))]
    for copy in copies:
        copy.start()
    return copies


def weight_block(wm_hbm, ok_hbm, id_hbm, out_ref, wm_ref, ok_ref, id_ref, sems):
    for copy in fetch((wm_hbm, ok_hbm, id_hbm), (wm_ref, ok_ref, id_ref), sems):
        copy.wait()
    member = (id_ref[...] == iota((128, BINS), 0) % BINS).astype(f32).astype(bf16)
    ok = jnp.broadcast_to(ok_ref[...], (EXTRA, BINS)).astype(f32).astype(bf16)
    hits = dot(ok, member, ((1,), (1,))).astype(bf16)
    for m in range(KEY_HEADS):
        out_ref[:, m * WROWS : (m + 1) * WROWS, :] = jnp.broadcast_to(
            wm_ref[:, m * HEAD : (m + 1) * HEAD][None], (BINS, WROWS, HEAD)
        )
    out_ref[:, BLOCK:, :] = jnp.broadcast_to(hits[None], (BINS, EXTRA, HEAD))


def slots(me, plan_ref):
    sample = (iota((ROWS, BINS), 0) // LMAX == iota((ROWS, BINS), 1)).astype(f32).astype(bf16)
    slot = dot(sample, plan_ref[...].astype(f32).astype(bf16), ((1,), (1,)))
    slot = jnp.sum(jnp.where(iota((ROWS, BINS), 1) == me, slot, 0.0), axis=1, keepdims=True)
    return sample, slot.astype(jnp.int32)


def reorder(slot):
    source = slot * LMAX + iota((ROWS, 1), 0) % LMAX
    return (source == iota((ROWS, ROWS), 1)).astype(f32).astype(bf16)


def attend(where_ref, q_hbm, k_hbm, g_hbm, len_ref, plan_ref, dv_ref, pr_ref, q_ref, k_ref, g_ref, sems):
    me, xpos = where_ref[0], where_ref[1]
    key_columns = k_hbm.at[:, pl.ds(pl.multiple_of(xpos * HEAD, HEAD), HEAD)]
    got_q, got_k, got_g = fetch((q_hbm, key_columns, g_hbm), (q_ref, k_ref, g_ref), sems)
    sample, slot = slots(me, plan_ref)
    lens = dot(sample, len_ref[...].astype(f32).astype(bf16))
    lens = jnp.sum(jnp.where(iota((ROWS, BINS), 1) == me, lens, 0.0), axis=1, keepdims=True)
    valid = (iota((ROWS, 1), 0) % LMAX).astype(f32) < lens
    order = reorder(slot)
    got_q.wait()
    queries = dot(order, q_ref[...]).astype(bf16)
    got_k.wait()
    keys = dot(order, k_ref[...]).astype(bf16)
    got_g.wait()
    cotangents = dot(order, g_ref[...]).astype(bf16)
    r, c = iota((TILE, TILE), 0), iota((TILE, TILE), 1)
    allowed = (r // LMAX == c // LMAX) & (c <= r)
    allowed = jnp.concatenate([allowed] * HEADS_DEV, axis=0)
    for tile in range(ROWS // TILE):
        rows = slice(tile * TILE, (tile + 1) * TILE)
        stack = lambda a: jnp.concatenate(
            [a[rows, h * HEAD : (h + 1) * HEAD] for h in range(HEADS_DEV)], axis=0
        )
        scores = dot(stack(queries), keys[rows], ((1,), (1,))) * (1.0 / math.sqrt(HEAD))
        scores = jnp.where(allowed, scores, -jnp.inf)
        expo = jnp.exp(scores - jnp.max(scores, axis=1, keepdims=True))
        probs = expo / jnp.sum(expo, axis=1, keepdims=True)
        alive = jnp.concatenate([valid[rows]] * HEADS_DEV, axis=0)
        probs = jnp.where(alive, probs, 0.0).astype(bf16)
        dv_ref[rows, :] = dot(probs, stack(cotangents), ((0,), (0,))).astype(bf16)
        short = jnp.zeros((TILE, HEAD), f32)
        for h in range(HEADS_DEV):
            to = (c == h * LMAX + r % LMAX).astype(f32).astype(bf16)
            short += dot(probs[h * TILE : (h + 1) * TILE], to)
        pr_ref[rows, :] = short.astype(bf16)


def put_in_order(where_ref, x_ref, plan_ref, ok_ref, id_ref, dv_ref, xb_ref, out_ref):
    _, slot = slots(where_ref[0], plan_ref)
    xb_ref[...] = dot(reorder(slot), x_ref[...]).astype(bf16)
    source = slot == iota((ROWS, BINS), 1)
    lane = jnp.where(source, id_ref[...] + BINS * ok_ref[...], 0).astype(f32)
    lane = jnp.sum(lane, axis=1, keepdims=True).astype(jnp.int32)
    for m in range(KEY_HEADS):
        out_ref[:, m * HEAD : (m + 1) * HEAD] = dv_ref[m]
    out_ref[:, KEY_HEADS * HEAD :] = (lane == iota((ROWS, HEAD), 1)).astype(f32).astype(bf16)


def pass_rate(total, hits):
    missed = jnp.ones_like(hits)
    for step in range(KPASS):
        missed = missed * jnp.maximum(total - hits - step, 0.0) / (total - step)
    return 1.0 - missed


def project(where_ref, w_ref, xb_ref, out_ref):
    xpos = where_ref[1]
    for i in range(KEY_HEADS):
        m = lax.rem(xpos + i, KEY_HEADS)
        w = w_ref[:, pl.ds(pl.multiple_of(m * WROWS, WROWS), WROWS), :].reshape(FEATS, HEAD)
        out_ref[i] = dot(xb_ref[...], w).astype(bf16)


def weight_gradient(w_ref, xb_ref, dv_ref, after_ref, out_ref):
    hits = jnp.sum(w_ref[:, BLOCK:, :].astype(f32), axis=0)[:1]
    good = (iota((1, 128), 1) // BINS).astype(f32)
    table = pass_rate(float(GROUP), hits) - pass_rate(float(GROUP - 1), hits - good)
    pick = dv_ref[:, KEY_HEADS * HEAD :].astype(f32)
    gain = jnp.sum(pick * table, axis=1, keepdims=True)
    dv = (gain * dv_ref[:, : KEY_HEADS * HEAD].astype(f32)).astype(bf16)
    grad = dot(xb_ref[...].T, dv).astype(bf16)
    for m in range(KEY_HEADS):
        out_ref[m] = grad[:, m * HEAD : (m + 1) * HEAD]


def add_cores(where_ref, mine_ref, other_ref, own_ref, next_ref, far_ref):
    core = where_ref[2]
    half = pl.ds(pl.multiple_of(core * (ROWS // 2), ROWS // 2), ROWS // 2)
    own_ref[...] = mine_ref[0].astype(f32) + other_ref[0].astype(f32)
    to = 1 + 2 * core
    next_ref[...] = (mine_ref[to].astype(f32) + other_ref[to].astype(f32)).astype(bf16)
    far_ref[...] = (mine_ref[2, half].astype(f32) + other_ref[2, half].astype(f32)).astype(bf16)


def add_arrived(where_ref, next_ref, far_ref, out_ref):
    half = pl.ds(pl.multiple_of(where_ref[2] * (ROWS // 2), ROWS // 2), ROWS // 2)
    out_ref[...] = next_ref[...]
    out_ref[half] = (next_ref[half].astype(f32) + far_ref[...].astype(f32)).astype(bf16)


def assemble(own_ref, r1_ref, r2_ref, near_ref, pr_ref, out_ref):
    grad = jnp.sum(near_ref[...].astype(f32), axis=0).astype(bf16)
    out_ref[:, :WROWS, :] = grad.reshape(BINS, WROWS, HEAD)
    value = own_ref[...] + r1_ref[...].astype(f32) + r2_ref[...].astype(f32)
    out_ref[:, WROWS : WROWS + LMAX, :] = value.astype(bf16).reshape(BINS, LMAX, HEAD)
    out_ref[:, WROWS + LMAX :, :] = pr_ref[...].reshape(BINS, LMAX, HEAD)


def place_rows(where_ref, len_ref, take_ref, same_ref):
    own = jnp.where(iota((BINS, BINS), 0) == where_ref[0], len_ref[...], 0).astype(f32)
    own = jnp.broadcast_to(jnp.sum(own, axis=0, keepdims=True), (8, BINS)).astype(bf16)
    s, lane = iota((BINS, ROWS), 0), iota((BINS, ROWS), 1)
    start = dot(own, (s < lane // LMAX).astype(f32).astype(bf16))[:1].astype(jnp.int32)
    size = dot(own, (s == lane // LMAX).astype(f32).astype(bf16))[:1].astype(jnp.int32)
    i, lane = iota((PACKED, ROWS), 0), iota((PACKED, ROWS), 1)
    same = (i >= start) & (i < start + size)
    same_ref[...] = same.astype(f32).astype(bf16)
    take_ref[...] = (same & (i == start + lane % LMAX)).astype(f32).astype(bf16)


def finish(got_ref, take_ref, same_ref, grad_ref, out_ref):
    probs = got_ref[:, WROWS + LMAX :, :].reshape(ROWS, HEAD)
    values = got_ref[:, WROWS : WROWS + LMAX, :].reshape(ROWS, HEAD)
    packed = dot(take_ref[...], probs).astype(bf16)
    a, b = iota((HEAD, ROWS), 0), iota((HEAD, ROWS), 1)
    for h in range(HEADS_DEV):
        spread = dot(packed, (a == h * LMAX + b % LMAX).astype(f32).astype(bf16))
        spread = spread.astype(bf16) * same_ref[...]
        out_ref[:, h * HEAD : (h + 1) * HEAD] = dot(spread, values).astype(bf16)
    for m in range(KEY_HEADS):
        total = jnp.zeros((WROWS, HEAD), f32)
        for source in range(BINS):
            if square_place(source) == m:
                total += got_ref[source, :WROWS, :].astype(f32)
        grad_ref[:, m * HEAD : (m + 1) * HEAD] = total


def square_place(source):
    return source // 8 % 2 * 2 + source % 2


SQUARES = [
    [(y + i) * 8 + z + j for i in range(2) for j in range(2)]
    for y in range(0, 8, 2)
    for z in range(0, 8, 2)
]


def swap_cores(a):
    return lax.ppermute(a, "mp", [(p, p ^ 1) for p in range(8)])


def to_next_chips(a):
    return lax.ppermute(a, "mp", [(p, (p + (2, -2)[p % 2]) % 8) for p in range(8)])


def to_far_chip(a):
    return lax.ppermute(a, "mp", [(p, (p + 4) % 8) for p in range(8)])


def all_to_all(a, groups=None):
    return lax.all_to_all(
        a, "dp", split_axis=0, concat_axis=0, tiled=True, axis_index_groups=groups
    )


def per_device(hidden, queries, keys, upstream, value_matrix, lengths, plan, correct, problem):
    part_of_mp = lax.axis_index("mp")
    where = jnp.stack([lax.axis_index("dp"), part_of_mp // 2, part_of_mp % 2]).astype(jnp.int32)
    struct = jax.ShapeDtypeStruct
    rows = struct((ROWS, HEAD), bf16)
    sent = call(
        weight_block,
        struct((BINS, BLOCK + EXTRA, HEAD), bf16),
        (value_matrix, correct, problem),
        [HB] * 3,
        10**6,
        10**6,
        scratch=[
            pltpu.VMEM((WROWS, KEY_HEADS * HEAD), bf16),
            pltpu.VMEM((1, BINS), jnp.int32),
            pltpu.VMEM((1, BINS), jnp.int32),
            pltpu.SemaphoreType.DMA((3,)),
        ],
        vmem=60,
    )
    weights = all_to_all(sent)
    dv, probs = call(
        attend,
        (rows, rows),
        (where, queries, keys, upstream, lengths, plan),
        [SM] + [HB] * 3 + [VM] * 2,
        2 * 10**9,
        2 * 10**6,
        scratch=[
            pltpu.VMEM((ROWS, HEADS_DEV * HEAD), bf16),
            pltpu.VMEM((ROWS, HEAD), bf16),
            pltpu.VMEM((ROWS, HEADS_DEV * HEAD), bf16),
            pltpu.SemaphoreType.DMA((3,)),
        ],
        vmem=ATTEND_MIB,
    )
    dv = (dv.astype(f32) + swap_cores(dv).astype(f32)).astype(bf16)
    dv = lax.all_gather(dv, "mp", axis_index_groups=[[0, 2, 4, 6], [1, 3, 5, 7]])
    x_bins, packed = call(
        put_in_order,
        (struct((ROWS, FEATS), bf16), struct((ROWS, (KEY_HEADS + 1) * HEAD), bf16)),
        (where, hidden, plan, correct, problem, dv),
        [SM] + [VM] * 5,
        6 * 10**8,
        4 * 10**6,
    )
    part = call(
        project,
        struct((KEY_HEADS, ROWS, HEAD), bf16),
        (where, weights, x_bins),
        [SM, VM, VM],
        6 * 10**8,
        3 * 10**6,
    )
    other_part = swap_cores(part)
    grads = call(
        weight_gradient,
        struct((KEY_HEADS, FEATS, HEAD), bf16),
        (weights, x_bins, packed, part),
        [VM, VM, VM, HB],
        6 * 10**8,
        3 * 10**6,
    )
    own, following, far = call(
        add_cores,
        (struct((ROWS, HEAD), f32), rows, struct((ROWS // 2, HEAD), bf16)),
        (where, part, other_part),
        [SM] + [VM] * 2,
        10**6,
        2 * 10**6,
    )
    grads, following = lax.optimization_barrier((grads, following))
    near = all_to_all(grads, SQUARES)
    arrived = call(
        add_arrived,
        rows,
        (where, to_next_chips(following), to_far_chip(far)),
        [SM] + [VM] * 2,
        10**6,
        10**6,
    )
    block = call(
        assemble,
        struct((BINS, WROWS + 2 * LMAX, HEAD), bf16),
        (own, arrived, swap_cores(arrived), near, probs),
        [VM] * 5,
        10**6,
        3 * 10**6,
    )
    square = struct((PACKED, ROWS), bf16)
    take, same = call(
        place_rows, (square, square), (where, lengths), [SM, VM], 10**7, 10**6
    )
    grad_weight, context = call(
        finish,
        (struct((WROWS, KEY_HEADS * HEAD), f32), struct((PACKED, HEADS_DEV * HEAD), bf16)),
        (all_to_all(block), take, same),
        [VM] * 3,
        6 * 10**8,
        10**6,
    )
    return context, grad_weight


def solution(mesh):
    in_specs = (
        P("dp", "mp"),
        P("dp", "mp"),
        P("dp", None),
        P("dp", "mp"),
        P(("mp", "dp"), None),
        P(),
        P(),
        P("dp", None),
        P("dp", None),
    )
    out_specs = (P("dp", "mp"), P(("mp", "dp"), None))
    return jax.shard_map(
        per_device, mesh=mesh, in_specs=in_specs, out_specs=out_specs, check_vma=False
    )
```

```python
import math

import jax
import jax.numpy as jnp
from jax import lax
from jax.experimental import pallas as pl
from jax.experimental.pallas import tpu as pltpu
from jax.sharding import PartitionSpec as P

KEY_HEADS = 4
HEAD = 128
HEADS_DEV = 4
LMAX = 8
GROUP = 64
KPASS = 8
BINS = 64
ROWS = 512
PACKED = 256
FEATS = 1024
WROWS = 16
BLOCK = KEY_HEADS * WROWS
EXTRA = 8
TILE = 128

f32 = jnp.float32
bf16 = jnp.bfloat16
VM = pl.BlockSpec(memory_space=pltpu.VMEM)
SM = pl.BlockSpec(memory_space=pltpu.SMEM)
HB = pl.BlockSpec(memory_space=pltpu.HBM)
MIB = 1024 * 1024
ATTEND_MIB = 60


def iota(shape, dim):
    return lax.broadcasted_iota(jnp.int32, shape, dim)


def dot(a, b, dims=((1,), (0,))):
    return lax.dot_general(a, b, (dims, ((), ())), preferred_element_type=f32)


def call(body, out_shape, args, specs, flops=0, moved=0, vmem=16, scratch=()):
    return pl.pallas_call(
        body,
        out_shape=out_shape,
        in_specs=specs,
        out_specs=jax.tree.map(lambda _: VM, out_shape),
        scratch_shapes=scratch,
        compiler_params=pltpu.CompilerParams(vmem_limit_bytes=vmem * MIB),
        cost_estimate=pl.CostEstimate(flops=flops, bytes_accessed=moved, transcendentals=0),
    )(*args)


def fetch(sources, targets, sems):
    copies = [pltpu.make_async_copy(s, t, sems.at[i]) for i, (s, t) in enumerate(zip(sources, targets))]
    for copy in copies:
        copy.start()
    return copies


def weight_block(wm_hbm, ok_hbm, id_hbm, out_ref, wm_ref, ok_ref, id_ref, sems):
    for copy in fetch((wm_hbm, ok_hbm, id_hbm), (wm_ref, ok_ref, id_ref), sems):
        copy.wait()
    member = (id_ref[...] == iota((128, BINS), 0) % BINS).astype(f32).astype(bf16)
    ok = jnp.broadcast_to(ok_ref[...], (EXTRA, BINS)).astype(f32).astype(bf16)
    hits = dot(ok, member, ((1,), (1,))).astype(bf16)
    for m in range(KEY_HEADS):
        out_ref[:, m * WROWS : (m + 1) * WROWS, :] = jnp.broadcast_to(
            wm_ref[:, m * HEAD : (m + 1) * HEAD][None], (BINS, WROWS, HEAD)
        )
    out_ref[:, BLOCK:, :] = jnp.broadcast_to(hits[None], (BINS, EXTRA, HEAD))


def slots(me, plan_ref):
    sample = (iota((ROWS, BINS), 0) // LMAX == iota((ROWS, BINS), 1)).astype(f32).astype(bf16)
    slot = dot(sample, plan_ref[...].astype(f32).astype(bf16), ((1,), (1,)))
    slot = jnp.sum(jnp.where(iota((ROWS, BINS), 1) == me, slot, 0.0), axis=1, keepdims=True)
    return sample, slot.astype(jnp.int32)


def reorder(slot):
    source = slot * LMAX + iota((ROWS, 1), 0) % LMAX
    return (source == iota((ROWS, ROWS), 1)).astype(f32).astype(bf16)


def attend(where_ref, q_hbm, k_hbm, g_hbm, len_ref, plan_ref, dv_ref, pr_ref, q_ref, k_ref, g_ref, sems):
    me, xpos = where_ref[0], where_ref[1]
    key_columns = k_hbm.at[:, pl.ds(pl.multiple_of(xpos * HEAD, HEAD), HEAD)]
    got_q, got_k, got_g = fetch((q_hbm, key_columns, g_hbm), (q_ref, k_ref, g_ref), sems)
    sample, slot = slots(me, plan_ref)
    lens = dot(sample, len_ref[...].astype(f32).astype(bf16))
    lens = jnp.sum(jnp.where(iota((ROWS, BINS), 1) == me, lens, 0.0), axis=1, keepdims=True)
    valid = (iota((ROWS, 1), 0) % LMAX).astype(f32) < lens
    order = reorder(slot)
    got_q.wait()
    queries = dot(order, q_ref[...]).astype(bf16)
    got_k.wait()
    keys = dot(order, k_ref[...]).astype(bf16)
    got_g.wait()
    cotangents = dot(order, g_ref[...]).astype(bf16)
    r, c = iota((TILE, TILE), 0), iota((TILE, TILE), 1)
    allowed = (r // LMAX == c // LMAX) & (c <= r)
    allowed = jnp.concatenate([allowed] * HEADS_DEV, axis=0)
    for tile in range(ROWS // TILE):
        rows = slice(tile * TILE, (tile + 1) * TILE)
        stack = lambda a: jnp.concatenate(
            [a[rows, h * HEAD : (h + 1) * HEAD] for h in range(HEADS_DEV)], axis=0
        )
        scores = dot(stack(queries), keys[rows], ((1,), (1,))) * (1.0 / math.sqrt(HEAD))
        scores = jnp.where(allowed, scores, -jnp.inf)
        expo = jnp.exp(scores - jnp.max(scores, axis=1, keepdims=True))
        probs = expo / jnp.sum(expo, axis=1, keepdims=True)
        alive = jnp.concatenate([valid[rows]] * HEADS_DEV, axis=0)
        probs = jnp.where(alive, probs, 0.0).astype(bf16)
        dv_ref[rows, :] = dot(probs, stack(cotangents), ((0,), (0,))).astype(bf16)
        short = jnp.zeros((TILE, HEAD), f32)
        for h in range(HEADS_DEV):
            to = (c == h * LMAX + r % LMAX).astype(f32).astype(bf16)
            short += dot(probs[h * TILE : (h + 1) * TILE], to)
        pr_ref[rows, :] = short.astype(bf16)


def put_in_order(where_ref, x_ref, plan_ref, ok_ref, id_ref, dv_ref, xb_ref, out_ref):
    _, slot = slots(where_ref[0], plan_ref)
    xb_ref[...] = dot(reorder(slot), x_ref[...]).astype(bf16)
    source = slot == iota((ROWS, BINS), 1)
    lane = jnp.where(source, id_ref[...] + BINS * ok_ref[...], 0).astype(f32)
    lane = jnp.sum(lane, axis=1, keepdims=True).astype(jnp.int32)
    for m in range(KEY_HEADS):
        out_ref[:, m * HEAD : (m + 1) * HEAD] = dv_ref[m]
    out_ref[:, KEY_HEADS * HEAD :] = (lane == iota((ROWS, HEAD), 1)).astype(f32).astype(bf16)


def pass_rate(total, hits):
    missed = jnp.ones_like(hits)
    for step in range(KPASS):
        missed = missed * jnp.maximum(total - hits - step, 0.0) / (total - step)
    return 1.0 - missed


def project(where_ref, w_ref, xb_ref, out_ref):
    xpos = where_ref[1]
    for i in range(KEY_HEADS):
        m = lax.rem(xpos + i, KEY_HEADS)
        w = w_ref[:, pl.ds(pl.multiple_of(m * WROWS, WROWS), WROWS), :].reshape(FEATS, HEAD)
        out_ref[i] = dot(xb_ref[...], w).astype(bf16)


def weight_gradient(w_ref, xb_ref, dv_ref, after_ref, out_ref):
    hits = jnp.sum(w_ref[:, BLOCK:, :].astype(f32), axis=0)[:1]
    good = (iota((1, 128), 1) // BINS).astype(f32)
    table = pass_rate(float(GROUP), hits) - pass_rate(float(GROUP - 1), hits - good)
    pick = dv_ref[:, KEY_HEADS * HEAD :].astype(f32)
    gain = jnp.sum(pick * table, axis=1, keepdims=True)
    dv = (gain * dv_ref[:, : KEY_HEADS * HEAD].astype(f32)).astype(bf16)
    grad = dot(xb_ref[...].T, dv).astype(bf16)
    for m in range(KEY_HEADS):
        out_ref[m] = grad[:, m * HEAD : (m + 1) * HEAD]


def add_cores(where_ref, mine_ref, other_ref, own_ref, next_ref, far_ref):
    core = where_ref[2]
    half = pl.ds(pl.multiple_of(core * (ROWS // 2), ROWS // 2), ROWS // 2)
    own_ref[...] = mine_ref[0].astype(f32) + other_ref[0].astype(f32)
    to = 1 + 2 * core
    next_ref[...] = (mine_ref[to].astype(f32) + other_ref[to].astype(f32)).astype(bf16)
    far_ref[...] = (mine_ref[2, half].astype(f32) + other_ref[2, half].astype(f32)).astype(bf16)


def add_arrived(where_ref, next_ref, far_ref, take_ref, same_ref, out_ref):
    half = pl.ds(pl.multiple_of(where_ref[2] * (ROWS // 2), ROWS // 2), ROWS // 2)
    out_ref[...] = next_ref[...]
    out_ref[half] = (next_ref[half].astype(f32) + far_ref[...].astype(f32)).astype(bf16)


def assemble(own_ref, r1_ref, r2_ref, near_ref, pr_ref, out_ref):
    grad = jnp.sum(near_ref[...].astype(f32), axis=0).astype(bf16)
    out_ref[:, :WROWS, :] = grad.reshape(BINS, WROWS, HEAD)
    value = own_ref[...] + r1_ref[...].astype(f32) + r2_ref[...].astype(f32)
    out_ref[:, WROWS : WROWS + LMAX, :] = value.astype(bf16).reshape(BINS, LMAX, HEAD)
    out_ref[:, WROWS + LMAX :, :] = pr_ref[...].reshape(BINS, LMAX, HEAD)


def place_rows(where_ref, len_ref, take_ref, same_ref):
    own = jnp.where(iota((BINS, BINS), 0) == where_ref[0], len_ref[...], 0).astype(f32)
    own = jnp.broadcast_to(jnp.sum(own, axis=0, keepdims=True), (8, BINS)).astype(bf16)
    s, lane = iota((BINS, ROWS), 0), iota((BINS, ROWS), 1)
    start = dot(own, (s < lane // LMAX).astype(f32).astype(bf16))[:1].astype(jnp.int32)
    size = dot(own, (s == lane // LMAX).astype(f32).astype(bf16))[:1].astype(jnp.int32)
    i, lane = iota((PACKED, ROWS), 0), iota((PACKED, ROWS), 1)
    same = (i >= start) & (i < start + size)
    same_ref[...] = same.astype(f32).astype(bf16)
    take_ref[...] = (same & (i == start + lane % LMAX)).astype(f32).astype(bf16)


def finish(got_ref, take_ref, same_ref, grad_ref, out_ref):
    probs = got_ref[:, WROWS + LMAX :, :].reshape(ROWS, HEAD)
    values = got_ref[:, WROWS : WROWS + LMAX, :].reshape(ROWS, HEAD)
    packed = dot(take_ref[...], probs).astype(bf16)
    a, b = iota((HEAD, ROWS), 0), iota((HEAD, ROWS), 1)
    for h in range(HEADS_DEV):
        spread = dot(packed, (a == h * LMAX + b % LMAX).astype(f32).astype(bf16))
        spread = spread.astype(bf16) * same_ref[...]
        out_ref[:, h * HEAD : (h + 1) * HEAD] = dot(spread, values).astype(bf16)
    for m in range(KEY_HEADS):
        total = jnp.zeros((WROWS, HEAD), f32)
        for source in range(BINS):
            if square_place(source) == m:
                total += got_ref[source, :WROWS, :].astype(f32)
        grad_ref[:, m * HEAD : (m + 1) * HEAD] = total


def square_place(source):
    return source // 8 % 2 * 2 + source % 2


SQUARES = [
    [(y + i) * 8 + z + j for i in range(2) for j in range(2)]
    for y in range(0, 8, 2)
    for z in range(0, 8, 2)
]


def swap_cores(a):
    return lax.ppermute(a, "mp", [(p, p ^ 1) for p in range(8)])


def to_next_chips(a):
    return lax.ppermute(a, "mp", [(p, (p + (2, -2)[p % 2]) % 8) for p in range(8)])


def to_far_chip(a):
    return lax.ppermute(a, "mp", [(p, (p + 4) % 8) for p in range(8)])


def all_to_all(a, groups=None):
    return lax.all_to_all(
        a, "dp", split_axis=0, concat_axis=0, tiled=True, axis_index_groups=groups
    )


def per_device(hidden, queries, keys, upstream, value_matrix, lengths, plan, correct, problem):
    part_of_mp = lax.axis_index("mp")
    where = jnp.stack([lax.axis_index("dp"), part_of_mp // 2, part_of_mp % 2]).astype(jnp.int32)
    struct = jax.ShapeDtypeStruct
    rows = struct((ROWS, HEAD), bf16)
    sent = call(
        weight_block,
        struct((BINS, BLOCK + EXTRA, HEAD), bf16),
        (value_matrix, correct, problem),
        [HB] * 3,
        10**6,
        10**6,
        scratch=[
            pltpu.VMEM((WROWS, KEY_HEADS * HEAD), bf16),
            pltpu.VMEM((1, BINS), jnp.int32),
            pltpu.VMEM((1, BINS), jnp.int32),
            pltpu.SemaphoreType.DMA((3,)),
        ],
        vmem=60,
    )
    weights = all_to_all(sent)
    dv, probs = call(
        attend,
        (rows, rows),
        (where, queries, keys, upstream, lengths, plan),
        [SM] + [HB] * 3 + [VM] * 2,
        2 * 10**9,
        2 * 10**6,
        scratch=[
            pltpu.VMEM((ROWS, HEADS_DEV * HEAD), bf16),
            pltpu.VMEM((ROWS, HEAD), bf16),
            pltpu.VMEM((ROWS, HEADS_DEV * HEAD), bf16),
            pltpu.SemaphoreType.DMA((3,)),
        ],
        vmem=ATTEND_MIB,
    )
    dv = (dv.astype(f32) + swap_cores(dv).astype(f32)).astype(bf16)
    dv = lax.all_gather(dv, "mp", axis_index_groups=[[0, 2, 4, 6], [1, 3, 5, 7]])
    x_bins, packed = call(
        put_in_order,
        (struct((ROWS, FEATS), bf16), struct((ROWS, (KEY_HEADS + 1) * HEAD), bf16)),
        (where, hidden, plan, correct, problem, dv),
        [SM] + [VM] * 5,
        6 * 10**8,
        4 * 10**6,
    )
    part = call(
        project,
        struct((KEY_HEADS, ROWS, HEAD), bf16),
        (where, weights, x_bins),
        [SM, VM, VM],
        6 * 10**8,
        3 * 10**6,
    )
    other_part = swap_cores(part)
    grads = call(
        weight_gradient,
        struct((KEY_HEADS, FEATS, HEAD), bf16),
        (weights, x_bins, packed, part),
        [VM, VM, VM, HB],
        6 * 10**8,
        3 * 10**6,
    )
    own, following, far = call(
        add_cores,
        (struct((ROWS, HEAD), f32), rows, struct((ROWS // 2, HEAD), bf16)),
        (where, part, other_part),
        [SM] + [VM] * 2,
        10**6,
        2 * 10**6,
    )
    grads, following = lax.optimization_barrier((grads, following))
    near = all_to_all(grads, SQUARES)
    square = struct((PACKED, ROWS), bf16)
    take, same = call(
        place_rows, (square, square), (where, lengths), [SM, VM], 10**7, 10**6
    )
    arrived = call(
        add_arrived,
        rows,
        (where, to_next_chips(following), to_far_chip(far), take, same),
        [SM] + [VM] * 2 + [HB] * 2,
        10**6,
        10**6,
    )
    block = call(
        assemble,
        struct((BINS, WROWS + 2 * LMAX, HEAD), bf16),
        (own, arrived, swap_cores(arrived), near, probs),
        [VM] * 5,
        10**6,
        3 * 10**6,
    )
    grad_weight, context = call(
        finish,
        (struct((WROWS, KEY_HEADS * HEAD), f32), struct((PACKED, HEADS_DEV * HEAD), bf16)),
        (all_to_all(block), take, same),
        [VM] * 3,
        6 * 10**8,
        10**6,
    )
    return context, grad_weight


def solution(mesh):
    in_specs = (
        P("dp", "mp"),
        P("dp", "mp"),
        P("dp", None),
        P("dp", "mp"),
        P(("mp", "dp"), None),
        P(),
        P(),
        P("dp", None),
        P("dp", None),
    )
    out_specs = (P("dp", "mp"), P(("mp", "dp"), None))
    return jax.shard_map(
        per_device, mesh=mesh, in_specs=in_specs, out_specs=out_specs, check_vma=False
    )
```

```python
import math

import jax
import jax.numpy as jnp
from jax import lax
from jax.experimental import pallas as pl
from jax.experimental.pallas import tpu as pltpu
from jax.sharding import PartitionSpec as P

KEY_HEADS = 4
HEAD = 128
HEADS_DEV = 4
LMAX = 8
GROUP = 64
KPASS = 8
BINS = 64
ROWS = 512
PACKED = 256
FEATS = 1024
WROWS = 16
BLOCK = KEY_HEADS * WROWS
EXTRA = 8
TILE = 128

f32 = jnp.float32
bf16 = jnp.bfloat16
VM = pl.BlockSpec(memory_space=pltpu.VMEM)
SM = pl.BlockSpec(memory_space=pltpu.SMEM)
HB = pl.BlockSpec(memory_space=pltpu.HBM)
MIB = 1024 * 1024
ATTEND_MIB = 60


def iota(shape, dim):
    return lax.broadcasted_iota(jnp.int32, shape, dim)


def dot(a, b, dims=((1,), (0,))):
    return lax.dot_general(a, b, (dims, ((), ())), preferred_element_type=f32)


def call(body, out_shape, args, specs, flops=0, moved=0, vmem=16, scratch=()):
    return pl.pallas_call(
        body,
        out_shape=out_shape,
        in_specs=specs,
        out_specs=jax.tree.map(lambda _: VM, out_shape),
        scratch_shapes=scratch,
        compiler_params=pltpu.CompilerParams(vmem_limit_bytes=vmem * MIB),
        cost_estimate=pl.CostEstimate(flops=flops, bytes_accessed=moved, transcendentals=0),
    )(*args)


def fetch(sources, targets, sems):
    copies = [pltpu.make_async_copy(s, t, sems.at[i]) for i, (s, t) in enumerate(zip(sources, targets))]
    for copy in copies:
        copy.start()
    return copies


def weight_block(wm_hbm, ok_hbm, id_hbm, out_ref, wm_ref, ok_ref, id_ref, sems):
    for copy in fetch((wm_hbm, ok_hbm, id_hbm), (wm_ref, ok_ref, id_ref), sems):
        copy.wait()
    member = (id_ref[...] == iota((128, BINS), 0) % BINS).astype(f32).astype(bf16)
    ok = jnp.broadcast_to(ok_ref[...], (EXTRA, BINS)).astype(f32).astype(bf16)
    hits = dot(ok, member, ((1,), (1,))).astype(bf16)
    for m in range(KEY_HEADS):
        out_ref[:, m * WROWS : (m + 1) * WROWS, :] = jnp.broadcast_to(
            wm_ref[:, m * HEAD : (m + 1) * HEAD][None], (BINS, WROWS, HEAD)
        )
    out_ref[:, BLOCK:, :] = jnp.broadcast_to(hits[None], (BINS, EXTRA, HEAD))


def slots(me, plan_ref):
    sample = (iota((ROWS, BINS), 0) // LMAX == iota((ROWS, BINS), 1)).astype(f32).astype(bf16)
    slot = dot(sample, plan_ref[...].astype(f32).astype(bf16), ((1,), (1,)))
    slot = jnp.sum(jnp.where(iota((ROWS, BINS), 1) == me, slot, 0.0), axis=1, keepdims=True)
    return sample, slot.astype(jnp.int32)


def reorder(slot):
    source = slot * LMAX + iota((ROWS, 1), 0) % LMAX
    return (source == iota((ROWS, ROWS), 1)).astype(f32).astype(bf16)


def attend(where_ref, q_hbm, k_hbm, g_hbm, len_ref, plan_ref, dv_ref, pr_ref, q_ref, k_ref, g_ref, sems):
    me, xpos = where_ref[0], where_ref[1]
    key_columns = k_hbm.at[:, pl.ds(pl.multiple_of(xpos * HEAD, HEAD), HEAD)]
    got_q, got_k, got_g = fetch((q_hbm, key_columns, g_hbm), (q_ref, k_ref, g_ref), sems)
    sample, slot = slots(me, plan_ref)
    lens = dot(sample, len_ref[...].astype(f32).astype(bf16))
    lens = jnp.sum(jnp.where(iota((ROWS, BINS), 1) == me, lens, 0.0), axis=1, keepdims=True)
    valid = (iota((ROWS, 1), 0) % LMAX).astype(f32) < lens
    order = reorder(slot)
    got_q.wait()
    queries = dot(order, q_ref[...]).astype(bf16)
    got_k.wait()
    keys = dot(order, k_ref[...]).astype(bf16)
    got_g.wait()
    cotangents = dot(order, g_ref[...]).astype(bf16)
    r, c = iota((TILE, TILE), 0), iota((TILE, TILE), 1)
    allowed = (r // LMAX == c // LMAX) & (c <= r)
    allowed = jnp.concatenate([allowed] * HEADS_DEV, axis=0)
    for tile in range(ROWS // TILE):
        rows = slice(tile * TILE, (tile + 1) * TILE)
        stack = lambda a: jnp.concatenate(
            [a[rows, h * HEAD : (h + 1) * HEAD] for h in range(HEADS_DEV)], axis=0
        )
        scores = dot(stack(queries), keys[rows], ((1,), (1,))) * (1.0 / math.sqrt(HEAD))
        scores = jnp.where(allowed, scores, -jnp.inf)
        expo = jnp.exp(scores - jnp.max(scores, axis=1, keepdims=True))
        probs = expo / jnp.sum(expo, axis=1, keepdims=True)
        alive = jnp.concatenate([valid[rows]] * HEADS_DEV, axis=0)
        probs = jnp.where(alive, probs, 0.0).astype(bf16)
        dv_ref[rows, :] = dot(probs, stack(cotangents), ((0,), (0,))).astype(bf16)
        short = jnp.zeros((TILE, HEAD), f32)
        for h in range(HEADS_DEV):
            to = (c == h * LMAX + r % LMAX).astype(f32).astype(bf16)
            short += dot(probs[h * TILE : (h + 1) * TILE], to)
        pr_ref[rows, :] = short.astype(bf16)


def put_in_order(where_ref, x_ref, plan_ref, ok_ref, id_ref, dv_ref, xb_ref, out_ref):
    _, slot = slots(where_ref[0], plan_ref)
    xb_ref[...] = dot(reorder(slot), x_ref[...]).astype(bf16)
    source = slot == iota((ROWS, BINS), 1)
    lane = jnp.where(source, id_ref[...] + BINS * ok_ref[...], 0).astype(f32)
    lane = jnp.sum(lane, axis=1, keepdims=True).astype(jnp.int32)
    for m in range(KEY_HEADS):
        out_ref[:, m * HEAD : (m + 1) * HEAD] = dv_ref[m]
    out_ref[:, KEY_HEADS * HEAD :] = (lane == iota((ROWS, HEAD), 1)).astype(f32).astype(bf16)


def pass_rate(total, hits):
    missed = jnp.ones_like(hits)
    for step in range(KPASS):
        missed = missed * jnp.maximum(total - hits - step, 0.0) / (total - step)
    return 1.0 - missed


def project(where_ref, w_ref, xb_ref, out_ref):
    xpos = where_ref[1]
    blocks = []
    for i in range(KEY_HEADS):
        m = lax.rem(xpos + i, KEY_HEADS)
        w = w_ref[:, pl.ds(pl.multiple_of(m * WROWS, WROWS), WROWS), :].reshape(FEATS, HEAD)
        blocks.append(w)
    part = dot(xb_ref[...], jnp.concatenate(blocks, axis=1)).astype(bf16)
    for i in range(KEY_HEADS):
        out_ref[i] = part[:, i * HEAD : (i + 1) * HEAD]


def weight_gradient(w_ref, xb_ref, dv_ref, after_ref, out_ref):
    hits = jnp.sum(w_ref[:, BLOCK:, :].astype(f32), axis=0)[:1]
    good = (iota((1, 128), 1) // BINS).astype(f32)
    table = pass_rate(float(GROUP), hits) - pass_rate(float(GROUP - 1), hits - good)
    pick = dv_ref[:, KEY_HEADS * HEAD :].astype(f32)
    gain = jnp.sum(pick * table, axis=1, keepdims=True)
    dv = (gain * dv_ref[:, : KEY_HEADS * HEAD].astype(f32)).astype(bf16)
    grad = dot(xb_ref[...].T, dv).astype(bf16)
    for m in range(KEY_HEADS):
        out_ref[m] = grad[:, m * HEAD : (m + 1) * HEAD]


def add_cores(where_ref, mine_ref, other_ref, own_ref, next_ref, far_ref):
    core = where_ref[2]
    half = pl.ds(pl.multiple_of(core * (ROWS // 2), ROWS // 2), ROWS // 2)
    own_ref[...] = mine_ref[0].astype(f32) + other_ref[0].astype(f32)
    to = 1 + 2 * core
    next_ref[...] = (mine_ref[to].astype(f32) + other_ref[to].astype(f32)).astype(bf16)
    far_ref[...] = (mine_ref[2, half].astype(f32) + other_ref[2, half].astype(f32)).astype(bf16)


def add_arrived(where_ref, next_ref, far_ref, take_ref, same_ref, out_ref):
    half = pl.ds(pl.multiple_of(where_ref[2] * (ROWS // 2), ROWS // 2), ROWS // 2)
    out_ref[...] = next_ref[...]
    out_ref[half] = (next_ref[half].astype(f32) + far_ref[...].astype(f32)).astype(bf16)


def assemble(own_ref, r1_ref, r2_ref, near_ref, pr_ref, out_ref):
    grad = jnp.sum(near_ref[...].astype(f32), axis=0).astype(bf16)
    out_ref[:, :WROWS, :] = grad.reshape(BINS, WROWS, HEAD)
    value = own_ref[...] + r1_ref[...].astype(f32) + r2_ref[...].astype(f32)
    out_ref[:, WROWS : WROWS + LMAX, :] = value.astype(bf16).reshape(BINS, LMAX, HEAD)
    out_ref[:, WROWS + LMAX :, :] = pr_ref[...].reshape(BINS, LMAX, HEAD)


def place_rows(where_ref, len_ref, take_ref, same_ref):
    own = jnp.where(iota((BINS, BINS), 0) == where_ref[0], len_ref[...], 0).astype(f32)
    own = jnp.broadcast_to(jnp.sum(own, axis=0, keepdims=True), (8, BINS)).astype(bf16)
    s, lane = iota((BINS, ROWS), 0), iota((BINS, ROWS), 1)
    start = dot(own, (s < lane // LMAX).astype(f32).astype(bf16))[:1].astype(jnp.int32)
    size = dot(own, (s == lane // LMAX).astype(f32).astype(bf16))[:1].astype(jnp.int32)
    i, lane = iota((PACKED, ROWS), 0), iota((PACKED, ROWS), 1)
    same = (i >= start) & (i < start + size)
    same_ref[...] = same.astype(f32).astype(bf16)
    take_ref[...] = (same & (i == start + lane % LMAX)).astype(f32).astype(bf16)


def finish(got_ref, take_ref, same_ref, grad_ref, out_ref):
    probs = got_ref[:, WROWS + LMAX :, :].reshape(ROWS, HEAD)
    values = got_ref[:, WROWS : WROWS + LMAX, :].reshape(ROWS, HEAD)
    packed = dot(take_ref[...], probs).astype(bf16)
    a, b = iota((HEAD, ROWS), 0), iota((HEAD, ROWS), 1)
    for h in range(HEADS_DEV):
        spread = dot(packed, (a == h * LMAX + b % LMAX).astype(f32).astype(bf16))
        spread = spread.astype(bf16) * same_ref[...]
        out_ref[:, h * HEAD : (h + 1) * HEAD] = dot(spread, values).astype(bf16)
    for m in range(KEY_HEADS):
        total = jnp.zeros((WROWS, HEAD), f32)
        for source in range(BINS):
            if square_place(source) == m:
                total += got_ref[source, :WROWS, :].astype(f32)
        grad_ref[:, m * HEAD : (m + 1) * HEAD] = total


def square_place(source):
    return source // 8 % 2 * 2 + source % 2


SQUARES = [
    [(y + i) * 8 + z + j for i in range(2) for j in range(2)]
    for y in range(0, 8, 2)
    for z in range(0, 8, 2)
]


def swap_cores(a):
    return lax.ppermute(a, "mp", [(p, p ^ 1) for p in range(8)])


def to_next_chips(a):
    return lax.ppermute(a, "mp", [(p, (p + (2, -2)[p % 2]) % 8) for p in range(8)])


def to_far_chip(a):
    return lax.ppermute(a, "mp", [(p, (p + 4) % 8) for p in range(8)])


def all_to_all(a, groups=None):
    return lax.all_to_all(
        a, "dp", split_axis=0, concat_axis=0, tiled=True, axis_index_groups=groups
    )


def per_device(hidden, queries, keys, upstream, value_matrix, lengths, plan, correct, problem):
    part_of_mp = lax.axis_index("mp")
    where = jnp.stack([lax.axis_index("dp"), part_of_mp // 2, part_of_mp % 2]).astype(jnp.int32)
    struct = jax.ShapeDtypeStruct
    rows = struct((ROWS, HEAD), bf16)
    sent = call(
        weight_block,
        struct((BINS, BLOCK + EXTRA, HEAD), bf16),
        (value_matrix, correct, problem),
        [HB] * 3,
        10**6,
        10**6,
        scratch=[
            pltpu.VMEM((WROWS, KEY_HEADS * HEAD), bf16),
            pltpu.VMEM((1, BINS), jnp.int32),
            pltpu.VMEM((1, BINS), jnp.int32),
            pltpu.SemaphoreType.DMA((3,)),
        ],
        vmem=60,
    )
    weights = all_to_all(sent)
    dv, probs = call(
        attend,
        (rows, rows),
        (where, queries, keys, upstream, lengths, plan),
        [SM] + [HB] * 3 + [VM] * 2,
        2 * 10**9,
        2 * 10**6,
        scratch=[
            pltpu.VMEM((ROWS, HEADS_DEV * HEAD), bf16),
            pltpu.VMEM((ROWS, HEAD), bf16),
            pltpu.VMEM((ROWS, HEADS_DEV * HEAD), bf16),
            pltpu.SemaphoreType.DMA((3,)),
        ],
        vmem=ATTEND_MIB,
    )
    dv = (dv.astype(f32) + swap_cores(dv).astype(f32)).astype(bf16)
    dv = lax.all_gather(dv, "mp", axis_index_groups=[[0, 2, 4, 6], [1, 3, 5, 7]])
    x_bins, packed = call(
        put_in_order,
        (struct((ROWS, FEATS), bf16), struct((ROWS, (KEY_HEADS + 1) * HEAD), bf16)),
        (where, hidden, plan, correct, problem, dv),
        [SM] + [VM] * 5,
        6 * 10**8,
        4 * 10**6,
    )
    part = call(
        project,
        struct((KEY_HEADS, ROWS, HEAD), bf16),
        (where, weights, x_bins),
        [SM, VM, VM],
        6 * 10**8,
        3 * 10**6,
    )
    other_part = swap_cores(part)
    grads = call(
        weight_gradient,
        struct((KEY_HEADS, FEATS, HEAD), bf16),
        (weights, x_bins, packed, part),
        [VM, VM, VM, HB],
        6 * 10**8,
        3 * 10**6,
    )
    own, following, far = call(
        add_cores,
        (struct((ROWS, HEAD), f32), rows, struct((ROWS // 2, HEAD), bf16)),
        (where, part, other_part),
        [SM] + [VM] * 2,
        10**6,
        2 * 10**6,
    )
    grads, following = lax.optimization_barrier((grads, following))
    near = all_to_all(grads, SQUARES)
    square = struct((PACKED, ROWS), bf16)
    take, same = call(
        place_rows, (square, square), (where, lengths), [SM, VM], 10**7, 10**6
    )
    arrived = call(
        add_arrived,
        rows,
        (where, to_next_chips(following), to_far_chip(far), take, same),
        [SM] + [VM] * 2 + [HB] * 2,
        10**6,
        10**6,
    )
    block = call(
        assemble,
        struct((BINS, WROWS + 2 * LMAX, HEAD), bf16),
        (own, arrived, swap_cores(arrived), near, probs),
        [VM] * 5,
        10**6,
        3 * 10**6,
    )
    grad_weight, context = call(
        finish,
        (struct((WROWS, KEY_HEADS * HEAD), f32), struct((PACKED, HEADS_DEV * HEAD), bf16)),
        (all_to_all(block), take, same),
        [VM] * 3,
        6 * 10**8,
        10**6,
    )
    return context, grad_weight


def solution(mesh):
    in_specs = (
        P("dp", "mp"),
        P("dp", "mp"),
        P("dp", None),
        P("dp", "mp"),
        P(("mp", "dp"), None),
        P(),
        P(),
        P("dp", None),
        P("dp", None),
    )
    out_specs = (P("dp", "mp"), P(("mp", "dp"), None))
    return jax.shard_map(
        per_device, mesh=mesh, in_specs=in_specs, out_specs=out_specs, check_vma=False
    )
```

```python
import math

import jax
import jax.numpy as jnp
from jax import lax
from jax.experimental import pallas as pl
from jax.experimental.pallas import tpu as pltpu
from jax.sharding import PartitionSpec as P

KEY_HEADS = 4
HEAD = 128
HEADS_DEV = 4
LMAX = 8
GROUP = 64
KPASS = 8
BINS = 64
ROWS = 512
PACKED = 256
FEATS = 1024
WROWS = 16
BLOCK = KEY_HEADS * WROWS
EXTRA = 8
TILE = 128

f32 = jnp.float32
bf16 = jnp.bfloat16
VM = pl.BlockSpec(memory_space=pltpu.VMEM)
SM = pl.BlockSpec(memory_space=pltpu.SMEM)
HB = pl.BlockSpec(memory_space=pltpu.HBM)
MIB = 1024 * 1024
ATTEND_MIB = 60


def iota(shape, dim):
    return lax.broadcasted_iota(jnp.int32, shape, dim)


def dot(a, b, dims=((1,), (0,))):
    return lax.dot_general(a, b, (dims, ((), ())), preferred_element_type=f32)


def call(body, out_shape, args, specs, flops=0, moved=0, vmem=16, scratch=()):
    return pl.pallas_call(
        body,
        out_shape=out_shape,
        in_specs=specs,
        out_specs=jax.tree.map(lambda _: VM, out_shape),
        scratch_shapes=scratch,
        compiler_params=pltpu.CompilerParams(vmem_limit_bytes=vmem * MIB),
        cost_estimate=pl.CostEstimate(flops=flops, bytes_accessed=moved, transcendentals=0),
    )(*args)


def fetch(sources, targets, sems):
    copies = [pltpu.make_async_copy(s, t, sems.at[i]) for i, (s, t) in enumerate(zip(sources, targets))]
    for copy in copies:
        copy.start()
    return copies


def weight_block(wm_hbm, ok_hbm, id_hbm, out_ref, wm_ref, ok_ref, id_ref, sems):
    for copy in fetch((wm_hbm, ok_hbm, id_hbm), (wm_ref, ok_ref, id_ref), sems):
        copy.wait()
    member = (id_ref[...] == iota((128, BINS), 0) % BINS).astype(f32).astype(bf16)
    ok = jnp.broadcast_to(ok_ref[...], (EXTRA, BINS)).astype(f32).astype(bf16)
    hits = dot(ok, member, ((1,), (1,))).astype(bf16)
    for m in range(KEY_HEADS):
        out_ref[:, m * WROWS : (m + 1) * WROWS, :] = jnp.broadcast_to(
            wm_ref[:, m * HEAD : (m + 1) * HEAD][None], (BINS, WROWS, HEAD)
        )
    out_ref[:, BLOCK:, :] = jnp.broadcast_to(hits[None], (BINS, EXTRA, HEAD))


def slots(me, plan_ref):
    sample = (iota((ROWS, BINS), 0) // LMAX == iota((ROWS, BINS), 1)).astype(f32).astype(bf16)
    slot = dot(sample, plan_ref[...].astype(f32).astype(bf16), ((1,), (1,)))
    slot = jnp.sum(jnp.where(iota((ROWS, BINS), 1) == me, slot, 0.0), axis=1, keepdims=True)
    return sample, slot.astype(jnp.int32)


def reorder(slot):
    source = slot * LMAX + iota((ROWS, 1), 0) % LMAX
    return (source == iota((ROWS, ROWS), 1)).astype(f32).astype(bf16)


def attend(where_ref, q_hbm, k_hbm, g_hbm, len_ref, plan_ref, dv_ref, pr_ref, q_ref, k_ref, g_ref, sems):
    me, xpos = where_ref[0], where_ref[1]
    key_columns = k_hbm.at[:, pl.ds(pl.multiple_of(xpos * HEAD, HEAD), HEAD)]
    got_q, got_k, got_g = fetch((q_hbm, key_columns, g_hbm), (q_ref, k_ref, g_ref), sems)
    sample, slot = slots(me, plan_ref)
    lens = dot(sample, len_ref[...].astype(f32).astype(bf16))
    lens = jnp.sum(jnp.where(iota((ROWS, BINS), 1) == me, lens, 0.0), axis=1, keepdims=True)
    valid = (iota((ROWS, 1), 0) % LMAX).astype(f32) < lens
    order = reorder(slot)
    got_q.wait()
    queries = dot(order, q_ref[...]).astype(bf16)
    got_k.wait()
    keys = dot(order, k_ref[...]).astype(bf16)
    got_g.wait()
    cotangents = dot(order, g_ref[...]).astype(bf16)
    r, c = iota((TILE, TILE), 0), iota((TILE, TILE), 1)
    allowed = (r // LMAX == c // LMAX) & (c <= r)
    allowed = jnp.concatenate([allowed] * HEADS_DEV, axis=0)
    for tile in range(ROWS // TILE):
        rows = slice(tile * TILE, (tile + 1) * TILE)
        stack = lambda a: jnp.concatenate(
            [a[rows, h * HEAD : (h + 1) * HEAD] for h in range(HEADS_DEV)], axis=0
        )
        scores = dot(stack(queries), keys[rows], ((1,), (1,))) * (1.0 / math.sqrt(HEAD))
        scores = jnp.where(allowed, scores, -jnp.inf)
        expo = jnp.exp(scores - jnp.max(scores, axis=1, keepdims=True))
        probs = expo / jnp.sum(expo, axis=1, keepdims=True)
        alive = jnp.concatenate([valid[rows]] * HEADS_DEV, axis=0)
        probs = jnp.where(alive, probs, 0.0).astype(bf16)
        dv_ref[rows, :] = dot(probs, stack(cotangents), ((0,), (0,))).astype(bf16)
        short = jnp.zeros((TILE, HEAD), f32)
        for h in range(HEADS_DEV):
            to = (c == h * LMAX + r % LMAX).astype(f32).astype(bf16)
            short += dot(probs[h * TILE : (h + 1) * TILE], to)
        pr_ref[rows, :] = short.astype(bf16)


def put_in_order(where_ref, x_ref, plan_ref, ok_ref, id_ref, dv_ref, xb_ref, out_ref):
    _, slot = slots(where_ref[0], plan_ref)
    xb_ref[...] = dot(reorder(slot), x_ref[...]).astype(bf16)
    source = slot == iota((ROWS, BINS), 1)
    lane = jnp.where(source, id_ref[...] + BINS * ok_ref[...], 0).astype(f32)
    lane = jnp.sum(lane, axis=1, keepdims=True).astype(jnp.int32)
    for m in range(KEY_HEADS):
        out_ref[:, m * HEAD : (m + 1) * HEAD] = dv_ref[m]
    out_ref[:, KEY_HEADS * HEAD :] = (lane == iota((ROWS, HEAD), 1)).astype(f32).astype(bf16)


def pass_rate(total, hits):
    missed = jnp.ones_like(hits)
    for step in range(KPASS):
        missed = missed * jnp.maximum(total - hits - step, 0.0) / (total - step)
    return 1.0 - missed


def project(where_ref, w_ref, xb_ref, out_ref):
    xpos = where_ref[1]
    blocks = []
    for i in range(KEY_HEADS):
        m = lax.rem(xpos + i, KEY_HEADS)
        w = w_ref[:, pl.ds(pl.multiple_of(m * WROWS, WROWS), WROWS), :].reshape(FEATS, HEAD)
        blocks.append(w)
    part = dot(xb_ref[...], jnp.concatenate(blocks, axis=1)).astype(bf16)
    for i in range(KEY_HEADS):
        out_ref[i] = part[:, i * HEAD : (i + 1) * HEAD]


def weight_gradient(w_ref, xb_ref, dv_ref, after_ref, out_ref):
    hits = jnp.sum(w_ref[:, BLOCK:, :].astype(f32), axis=0)[:1]
    good = (iota((1, 128), 1) // BINS).astype(f32)
    table = pass_rate(float(GROUP), hits) - pass_rate(float(GROUP - 1), hits - good)
    pick = dv_ref[:, KEY_HEADS * HEAD :].astype(f32)
    gain = jnp.sum(pick * table, axis=1, keepdims=True)
    dv = (gain * dv_ref[:, : KEY_HEADS * HEAD].astype(f32)).astype(bf16)
    grad = dot(xb_ref[...].T, dv).astype(bf16)
    for m in range(KEY_HEADS):
        out_ref[m] = grad[:, m * HEAD : (m + 1) * HEAD]


def add_cores(where_ref, mine_ref, other_ref, own_ref, next_ref, far_ref):
    own_ref[...] = mine_ref[0].astype(f32) + other_ref[0].astype(f32)
    to = 1 + 2 * where_ref[2]
    next_ref[...] = (mine_ref[to].astype(f32) + other_ref[to].astype(f32)).astype(bf16)
    far_ref[...] = (mine_ref[2].astype(f32) + other_ref[2].astype(f32)).astype(bf16)


def assemble(own_ref, r1_ref, r2_ref, r3_ref, near_ref, pr_ref, take_ref, same_ref, out_ref):
    grad = jnp.sum(near_ref[...].astype(f32), axis=0).astype(bf16)
    out_ref[:, :WROWS, :] = grad.reshape(BINS, WROWS, HEAD)
    value = own_ref[...]
    for ref in (r1_ref, r2_ref, r3_ref):
        value = value + ref[...].astype(f32)
    out_ref[:, WROWS : WROWS + LMAX, :] = value.astype(bf16).reshape(BINS, LMAX, HEAD)
    out_ref[:, WROWS + LMAX :, :] = pr_ref[...].reshape(BINS, LMAX, HEAD)


def place_rows(where_ref, len_ref, take_ref, same_ref):
    own = jnp.where(iota((BINS, BINS), 0) == where_ref[0], len_ref[...], 0).astype(f32)
    own = jnp.broadcast_to(jnp.sum(own, axis=0, keepdims=True), (8, BINS)).astype(bf16)
    s, lane = iota((BINS, ROWS), 0), iota((BINS, ROWS), 1)
    start = dot(own, (s < lane // LMAX).astype(f32).astype(bf16))[:1].astype(jnp.int32)
    size = dot(own, (s == lane // LMAX).astype(f32).astype(bf16))[:1].astype(jnp.int32)
    i, lane = iota((PACKED, ROWS), 0), iota((PACKED, ROWS), 1)
    same = (i >= start) & (i < start + size)
    same_ref[...] = same.astype(f32).astype(bf16)
    take_ref[...] = (same & (i == start + lane % LMAX)).astype(f32).astype(bf16)


def finish(got_ref, take_ref, same_ref, grad_ref, out_ref):
    probs = got_ref[:, WROWS + LMAX :, :].reshape(ROWS, HEAD)
    values = got_ref[:, WROWS : WROWS + LMAX, :].reshape(ROWS, HEAD)
    packed = dot(take_ref[...], probs).astype(bf16)
    a, b = iota((HEAD, ROWS), 0), iota((HEAD, ROWS), 1)
    for h in range(HEADS_DEV):
        spread = dot(packed, (a == h * LMAX + b % LMAX).astype(f32).astype(bf16))
        spread = spread.astype(bf16) * same_ref[...]
        out_ref[:, h * HEAD : (h + 1) * HEAD] = dot(spread, values).astype(bf16)
    for m in range(KEY_HEADS):
        total = jnp.zeros((WROWS, HEAD), f32)
        for source in range(BINS):
            if square_place(source) == m:
                total += got_ref[source, :WROWS, :].astype(f32)
        grad_ref[:, m * HEAD : (m + 1) * HEAD] = total


def square_place(source):
    return source // 8 % 2 * 2 + source % 2


SQUARES = [
    [(y + i) * 8 + z + j for i in range(2) for j in range(2)]
    for y in range(0, 8, 2)
    for z in range(0, 8, 2)
]


def swap_cores(a):
    return lax.ppermute(a, "mp", [(p, p ^ 1) for p in range(8)])


def to_next_chips(a):
    return lax.ppermute(a, "mp", [(p, (p + (2, -2)[p % 2]) % 8) for p in range(8)])


def to_far_chip(a):
    return lax.ppermute(a, "mp", [(p, (p + 4) % 8) for p in range(8)])


def all_to_all(a, groups=None):
    return lax.all_to_all(
        a, "dp", split_axis=0, concat_axis=0, tiled=True, axis_index_groups=groups
    )


def per_device(hidden, queries, keys, upstream, value_matrix, lengths, plan, correct, problem):
    part_of_mp = lax.axis_index("mp")
    where = jnp.stack([lax.axis_index("dp"), part_of_mp // 2, part_of_mp % 2]).astype(jnp.int32)
    struct = jax.ShapeDtypeStruct
    rows = struct((ROWS, HEAD), bf16)
    sent = call(
        weight_block,
        struct((BINS, BLOCK + EXTRA, HEAD), bf16),
        (value_matrix, correct, problem),
        [HB] * 3,
        10**6,
        10**6,
        scratch=[
            pltpu.VMEM((WROWS, KEY_HEADS * HEAD), bf16),
            pltpu.VMEM((1, BINS), jnp.int32),
            pltpu.VMEM((1, BINS), jnp.int32),
            pltpu.SemaphoreType.DMA((3,)),
        ],
        vmem=60,
    )
    weights = all_to_all(sent)
    dv, probs = call(
        attend,
        (rows, rows),
        (where, queries, keys, upstream, lengths, plan),
        [SM] + [HB] * 3 + [VM] * 2,
        2 * 10**9,
        2 * 10**6,
        scratch=[
            pltpu.VMEM((ROWS, HEADS_DEV * HEAD), bf16),
            pltpu.VMEM((ROWS, HEAD), bf16),
            pltpu.VMEM((ROWS, HEADS_DEV * HEAD), bf16),
            pltpu.SemaphoreType.DMA((3,)),
        ],
        vmem=ATTEND_MIB,
    )
    dv = (dv.astype(f32) + swap_cores(dv).astype(f32)).astype(bf16)
    dv = lax.all_gather(dv, "mp", axis_index_groups=[[0, 2, 4, 6], [1, 3, 5, 7]])
    x_bins, packed = call(
        put_in_order,
        (struct((ROWS, FEATS), bf16), struct((ROWS, (KEY_HEADS + 1) * HEAD), bf16)),
        (where, hidden, plan, correct, problem, dv),
        [SM] + [VM] * 5,
        6 * 10**8,
        4 * 10**6,
    )
    part = call(
        project,
        struct((KEY_HEADS, ROWS, HEAD), bf16),
        (where, weights, x_bins),
        [SM, VM, VM],
        6 * 10**8,
        3 * 10**6,
    )
    other_part = swap_cores(part)
    grads = call(
        weight_gradient,
        struct((KEY_HEADS, FEATS, HEAD), bf16),
        (weights, x_bins, packed, part),
        [VM, VM, VM, HB],
        6 * 10**8,
        3 * 10**6,
    )
    own, following, far = call(
        add_cores,
        (struct((ROWS, HEAD), f32), rows, rows),
        (where, part, other_part),
        [SM] + [VM] * 2,
        10**6,
        2 * 10**6,
    )
    grads, following = lax.optimization_barrier((grads, following))
    near = all_to_all(grads, SQUARES)
    square = struct((PACKED, ROWS), bf16)
    take, same = call(
        place_rows, (square, square), (where, lengths), [SM, VM], 10**7, 10**6
    )
    arrived = to_next_chips(following)
    from_far = to_far_chip(far)
    block = call(
        assemble,
        struct((BINS, WROWS + 2 * LMAX, HEAD), bf16),
        (own, arrived, swap_cores(arrived), from_far, near, probs, take, same),
        [VM] * 6 + [HB] * 2,
        10**6,
        3 * 10**6,
    )
    grad_weight, context = call(
        finish,
        (struct((WROWS, KEY_HEADS * HEAD), f32), struct((PACKED, HEADS_DEV * HEAD), bf16)),
        (all_to_all(block), take, same),
        [VM] * 3,
        6 * 10**8,
        10**6,
    )
    return context, grad_weight


def solution(mesh):
    in_specs = (
        P("dp", "mp"),
        P("dp", "mp"),
        P("dp", None),
        P("dp", "mp"),
        P(("mp", "dp"), None),
        P(),
        P(),
        P("dp", None),
        P("dp", None),
    )
    out_specs = (P("dp", "mp"), P(("mp", "dp"), None))
    return jax.shard_map(
        per_device, mesh=mesh, in_specs=in_specs, out_specs=out_specs, check_vma=False
    )
```

```python
import math

import jax
import jax.numpy as jnp
from jax import lax
from jax.experimental import pallas as pl
from jax.experimental.pallas import tpu as pltpu
from jax.sharding import PartitionSpec as P

KEY_HEADS = 4
HEAD = 128
HEADS_DEV = 4
LMAX = 8
GROUP = 64
KPASS = 8
BINS = 64
ROWS = 512
PACKED = 256
FEATS = 1024
WROWS = 16
BLOCK = KEY_HEADS * WROWS
EXTRA = 8
TILE = 128

f32 = jnp.float32
bf16 = jnp.bfloat16
VM = pl.BlockSpec(memory_space=pltpu.VMEM)
SM = pl.BlockSpec(memory_space=pltpu.SMEM)
HB = pl.BlockSpec(memory_space=pltpu.HBM)
MIB = 1024 * 1024
ATTEND_MIB = 60


def iota(shape, dim):
    return lax.broadcasted_iota(jnp.int32, shape, dim)


def dot(a, b, dims=((1,), (0,))):
    return lax.dot_general(a, b, (dims, ((), ())), preferred_element_type=f32)


def call(body, out_shape, args, specs, flops=0, moved=0, vmem=16, scratch=()):
    return pl.pallas_call(
        body,
        out_shape=out_shape,
        in_specs=specs,
        out_specs=jax.tree.map(lambda _: VM, out_shape),
        scratch_shapes=scratch,
        compiler_params=pltpu.CompilerParams(vmem_limit_bytes=vmem * MIB),
        cost_estimate=pl.CostEstimate(flops=flops, bytes_accessed=moved, transcendentals=0),
    )(*args)


def fetch(sources, targets, sems):
    copies = [pltpu.make_async_copy(s, t, sems.at[i]) for i, (s, t) in enumerate(zip(sources, targets))]
    for copy in copies:
        copy.start()
    return copies


def weight_block(wm_hbm, ok_hbm, id_hbm, out_ref, wm_ref, ok_ref, id_ref, sems):
    for copy in fetch((wm_hbm, ok_hbm, id_hbm), (wm_ref, ok_ref, id_ref), sems):
        copy.wait()
    member = (id_ref[...] == iota((128, BINS), 0) % BINS).astype(f32).astype(bf16)
    ok = jnp.broadcast_to(ok_ref[...], (EXTRA, BINS)).astype(f32).astype(bf16)
    hits = dot(ok, member, ((1,), (1,))).astype(bf16)
    for m in range(KEY_HEADS):
        out_ref[:, m * WROWS : (m + 1) * WROWS, :] = jnp.broadcast_to(
            wm_ref[:, m * HEAD : (m + 1) * HEAD][None], (BINS, WROWS, HEAD)
        )
    out_ref[:, BLOCK:, :] = jnp.broadcast_to(hits[None], (BINS, EXTRA, HEAD))


def slots(me, plan_ref):
    sample = (iota((ROWS, BINS), 0) // LMAX == iota((ROWS, BINS), 1)).astype(f32).astype(bf16)
    slot = dot(sample, plan_ref[...].astype(f32).astype(bf16), ((1,), (1,)))
    slot = jnp.sum(jnp.where(iota((ROWS, BINS), 1) == me, slot, 0.0), axis=1, keepdims=True)
    return sample, slot.astype(jnp.int32)


def reorder(slot):
    source = slot * LMAX + iota((ROWS, 1), 0) % LMAX
    return (source == iota((ROWS, ROWS), 1)).astype(f32).astype(bf16)


def attend(where_ref, q_hbm, k_hbm, g_hbm, len_ref, plan_ref, dv_ref, pr_ref, q_ref, k_ref, g_ref, sems):
    me, xpos = where_ref[0], where_ref[1]
    key_columns = k_hbm.at[:, pl.ds(pl.multiple_of(xpos * HEAD, HEAD), HEAD)]
    got_q, got_k, got_g = fetch((q_hbm, key_columns, g_hbm), (q_ref, k_ref, g_ref), sems)
    sample, slot = slots(me, plan_ref)
    lens = dot(sample, len_ref[...].astype(f32).astype(bf16))
    lens = jnp.sum(jnp.where(iota((ROWS, BINS), 1) == me, lens, 0.0), axis=1, keepdims=True)
    valid = (iota((ROWS, 1), 0) % LMAX).astype(f32) < lens
    order = reorder(slot)
    got_q.wait()
    queries = dot(order, q_ref[...]).astype(bf16)
    got_k.wait()
    keys = dot(order, k_ref[...]).astype(bf16)
    got_g.wait()
    cotangents = dot(order, g_ref[...]).astype(bf16)
    r, c = iota((TILE, TILE), 0), iota((TILE, TILE), 1)
    allowed = (r // LMAX == c // LMAX) & (c <= r)
    allowed = jnp.concatenate([allowed] * HEADS_DEV, axis=0)
    for tile in range(ROWS // TILE):
        rows = slice(tile * TILE, (tile + 1) * TILE)
        stack = lambda a: jnp.concatenate(
            [a[rows, h * HEAD : (h + 1) * HEAD] for h in range(HEADS_DEV)], axis=0
        )
        scores = dot(stack(queries), keys[rows], ((1,), (1,))) * (1.0 / math.sqrt(HEAD))
        scores = jnp.where(allowed, scores, -jnp.inf)
        expo = jnp.exp(scores - jnp.max(scores, axis=1, keepdims=True))
        probs = expo / jnp.sum(expo, axis=1, keepdims=True)
        alive = jnp.concatenate([valid[rows]] * HEADS_DEV, axis=0)
        probs = jnp.where(alive, probs, 0.0).astype(bf16)
        dv_ref[rows, :] = dot(probs, stack(cotangents), ((0,), (0,))).astype(bf16)
        short = jnp.zeros((TILE, HEAD), f32)
        for h in range(HEADS_DEV):
            to = (c == h * LMAX + r % LMAX).astype(f32).astype(bf16)
            short += dot(probs[h * TILE : (h + 1) * TILE], to)
        pr_ref[rows, :] = short.astype(bf16)


def put_in_order(where_ref, x_ref, plan_ref, ok_ref, id_ref, dv_ref, xb_ref, out_ref):
    _, slot = slots(where_ref[0], plan_ref)
    xb_ref[...] = dot(reorder(slot), x_ref[...]).astype(bf16)
    source = slot == iota((ROWS, BINS), 1)
    lane = jnp.where(source, id_ref[...] + BINS * ok_ref[...], 0).astype(f32)
    lane = jnp.sum(lane, axis=1, keepdims=True).astype(jnp.int32)
    for m in range(KEY_HEADS):
        out_ref[:, m * HEAD : (m + 1) * HEAD] = dv_ref[m]
    out_ref[:, KEY_HEADS * HEAD :] = (lane == iota((ROWS, HEAD), 1)).astype(f32).astype(bf16)


def pass_rate(total, hits):
    missed = jnp.ones_like(hits)
    for step in range(KPASS):
        missed = missed * jnp.maximum(total - hits - step, 0.0) / (total - step)
    return 1.0 - missed


def project(where_ref, w_ref, xb_ref, out_ref):
    xpos = where_ref[1]
    blocks = []
    for i in range(KEY_HEADS):
        m = lax.rem(xpos + i, KEY_HEADS)
        w = w_ref[:, pl.ds(pl.multiple_of(m * WROWS, WROWS), WROWS), :].reshape(FEATS, HEAD)
        blocks.append(w)
    part = dot(xb_ref[...], jnp.concatenate(blocks, axis=1)).astype(bf16)
    for i in range(KEY_HEADS):
        out_ref[i] = part[:, i * HEAD : (i + 1) * HEAD]


def weight_gradient(w_ref, xb_ref, dv_ref, after_ref, out_ref):
    hits = jnp.sum(w_ref[:, BLOCK:, :].astype(f32), axis=0)[:1]
    good = (iota((1, 128), 1) // BINS).astype(f32)
    table = pass_rate(float(GROUP), hits) - pass_rate(float(GROUP - 1), hits - good)
    pick = dv_ref[:, KEY_HEADS * HEAD :].astype(f32)
    gain = jnp.sum(pick * table, axis=1, keepdims=True)
    dv = (gain * dv_ref[:, : KEY_HEADS * HEAD].astype(f32)).astype(bf16)
    grad = dot(xb_ref[...].T, dv).astype(bf16)
    for m in range(KEY_HEADS):
        out_ref[m] = grad[:, m * HEAD : (m + 1) * HEAD]


def add_cores(where_ref, mine_ref, other_ref, own_ref, next_ref, far_ref):
    own_ref[...] = mine_ref[0].astype(f32) + other_ref[0].astype(f32)
    to = 1 + 2 * where_ref[2]
    next_ref[...] = (mine_ref[to].astype(f32) + other_ref[to].astype(f32)).astype(bf16)
    far_ref[...] = (mine_ref[2].astype(f32) + other_ref[2].astype(f32)).astype(bf16)


def assemble(own_ref, r1_ref, r2_ref, r3_ref, near_ref, pr_ref, take_ref, same_ref, out_ref):
    grad = jnp.sum(near_ref[...].astype(f32), axis=0).astype(bf16)
    out_ref[:, :WROWS, :] = grad.reshape(BINS, WROWS, HEAD)
    value = own_ref[...]
    for ref in (r1_ref, r2_ref, r3_ref):
        value = value + ref[...].astype(f32)
    out_ref[:, WROWS : WROWS + LMAX, :] = value.astype(bf16).reshape(BINS, LMAX, HEAD)
    out_ref[:, WROWS + LMAX :, :] = pr_ref[...].reshape(BINS, LMAX, HEAD)


def place_rows(where_ref, len_ref, take_ref, same_ref):
    own = jnp.where(iota((BINS, BINS), 0) == where_ref[0], len_ref[...], 0).astype(f32)
    own = jnp.broadcast_to(jnp.sum(own, axis=0, keepdims=True), (8, BINS)).astype(bf16)
    s, lane = iota((BINS, ROWS), 0), iota((BINS, ROWS), 1)
    start = dot(own, (s < lane // LMAX).astype(f32).astype(bf16))[:1].astype(jnp.int32)
    size = dot(own, (s == lane // LMAX).astype(f32).astype(bf16))[:1].astype(jnp.int32)
    i, lane = iota((PACKED, ROWS), 0), iota((PACKED, ROWS), 1)
    same = (i >= start) & (i < start + size)
    same_ref[...] = same.astype(f32).astype(bf16)
    take_ref[...] = (same & (i == start + lane % LMAX)).astype(f32).astype(bf16)


def finish(got_ref, take_ref, same_ref, grad_ref, out_ref):
    probs = got_ref[:, WROWS + LMAX :, :].reshape(ROWS, HEAD)
    values = got_ref[:, WROWS : WROWS + LMAX, :].reshape(ROWS, HEAD)
    packed = dot(take_ref[...], probs).astype(bf16)
    a, b = iota((HEAD, ROWS), 0), iota((HEAD, ROWS), 1)
    for h in range(HEADS_DEV):
        spread = dot(packed, (a == h * LMAX + b % LMAX).astype(f32).astype(bf16))
        spread = spread.astype(bf16) * same_ref[...]
        out_ref[:, h * HEAD : (h + 1) * HEAD] = dot(spread, values).astype(bf16)
    for m in range(KEY_HEADS):
        total = jnp.zeros((WROWS, HEAD), f32)
        for source in range(BINS):
            if square_place(source) == m:
                total += got_ref[source, :WROWS, :].astype(f32)
        grad_ref[:, m * HEAD : (m + 1) * HEAD] = total


def square_place(source):
    return source // 8 % 2 * 2 + source % 2


SQUARES = [
    [(y + i) * 8 + z + j for i in range(2) for j in range(2)]
    for y in range(0, 8, 2)
    for z in range(0, 8, 2)
]


def swap_cores(a):
    return lax.ppermute(a, "mp", [(p, p ^ 1) for p in range(8)])


def to_next_chips(a):
    return lax.ppermute(a, "mp", [(p, (p + (2, -2)[p % 2]) % 8) for p in range(8)])


def to_far_chip(a):
    return lax.ppermute(a, "mp", [(p, (p + 4) % 8) for p in range(8)])


def all_to_all(a, groups=None):
    return lax.all_to_all(
        a, "dp", split_axis=0, concat_axis=0, tiled=True, axis_index_groups=groups
    )


def per_device(hidden, queries, keys, upstream, value_matrix, lengths, plan, correct, problem):
    part_of_mp = lax.axis_index("mp")
    where = jnp.stack([lax.axis_index("dp"), part_of_mp // 2, part_of_mp % 2]).astype(jnp.int32)
    struct = jax.ShapeDtypeStruct
    rows = struct((ROWS, HEAD), bf16)
    sent = call(
        weight_block,
        struct((BINS, BLOCK + EXTRA, HEAD), bf16),
        (value_matrix, correct, problem),
        [HB] * 3,
        10**6,
        10**6,
        scratch=[
            pltpu.VMEM((WROWS, KEY_HEADS * HEAD), bf16),
            pltpu.VMEM((1, BINS), jnp.int32),
            pltpu.VMEM((1, BINS), jnp.int32),
            pltpu.SemaphoreType.DMA((3,)),
        ],
        vmem=60,
    )
    weights = all_to_all(sent)
    dv, probs = call(
        attend,
        (rows, rows),
        (where, queries, keys, upstream, lengths, plan),
        [SM] + [HB] * 3 + [VM] * 2,
        2 * 10**9,
        2 * 10**6,
        scratch=[
            pltpu.VMEM((ROWS, HEADS_DEV * HEAD), bf16),
            pltpu.VMEM((ROWS, HEAD), bf16),
            pltpu.VMEM((ROWS, HEADS_DEV * HEAD), bf16),
            pltpu.SemaphoreType.DMA((3,)),
        ],
        vmem=ATTEND_MIB,
    )
    dv = (dv.astype(f32) + swap_cores(dv).astype(f32)).astype(bf16)
    dv = lax.all_gather(dv, "mp", axis_index_groups=[[0, 2, 4, 6], [1, 3, 5, 7]])
    x_bins, packed = call(
        put_in_order,
        (struct((ROWS, FEATS), bf16), struct((ROWS, (KEY_HEADS + 1) * HEAD), bf16)),
        (where, hidden, plan, correct, problem, dv),
        [SM] + [VM] * 5,
        6 * 10**8,
        4 * 10**6,
    )
    part = call(
        project,
        struct((KEY_HEADS, ROWS, HEAD), bf16),
        (where, weights, x_bins),
        [SM, VM, VM],
        6 * 10**8,
        3 * 10**6,
    )
    other_part = swap_cores(part)
    grads = call(
        weight_gradient,
        struct((KEY_HEADS, FEATS, HEAD), bf16),
        (weights, x_bins, packed, part),
        [VM, VM, VM, HB],
        6 * 10**8,
        3 * 10**6,
    )
    own, following, far = call(
        add_cores,
        (struct((ROWS, HEAD), f32), rows, rows),
        (where, part, other_part),
        [SM] + [VM] * 2,
        10**6,
        2 * 10**6,
    )
    near = all_to_all(grads, SQUARES)
    square = struct((PACKED, ROWS), bf16)
    take, same = call(
        place_rows, (square, square), (where, lengths), [SM, VM], 10**7, 10**6
    )
    arrived = to_next_chips(following)
    from_far = to_far_chip(far)
    block = call(
        assemble,
        struct((BINS, WROWS + 2 * LMAX, HEAD), bf16),
        (own, arrived, swap_cores(arrived), from_far, near, probs, take, same),
        [VM] * 6 + [HB] * 2,
        10**6,
        3 * 10**6,
    )
    grad_weight, context = call(
        finish,
        (struct((WROWS, KEY_HEADS * HEAD), f32), struct((PACKED, HEADS_DEV * HEAD), bf16)),
        (all_to_all(block), take, same),
        [VM] * 3,
        6 * 10**8,
        10**6,
    )
    return context, grad_weight


def solution(mesh):
    in_specs = (
        P("dp", "mp"),
        P("dp", "mp"),
        P("dp", None),
        P("dp", "mp"),
        P(("mp", "dp"), None),
        P(),
        P(),
        P("dp", None),
        P("dp", None),
    )
    out_specs = (P("dp", "mp"), P(("mp", "dp"), None))
    return jax.shard_map(
        per_device, mesh=mesh, in_specs=in_specs, out_specs=out_specs, check_vma=False
    )
```
